32 devices in a mesh: rep: 2 (over y), tp: 8 (over z, x), grp: 2 (over core).
Axes of the slice: x: 2, y: 2, z: 4, core: 2. Of those that a mesh axis runs over, the one named last changes fastest.
Arguments:
- hidden: bfloat16 [1024, 28672], P(('rep', 'grp'), 'tp'), parts along dimension 0, may hold values from -6 to 6
- row_adapter_index: int32 [1024, 1], P(('rep', 'grp')), parts along dimension 0, may hold values from 0 to 15; in each aligned block of 256 rows (0 to 255, 256 to 511, ...) at most 64 rows name the same one
- down_projection_weight: bfloat16 [28672, 8192], P('tp'), may hold values from -0.046875 to 0.046875
- adapter_first_factor: bfloat16 [16, 28672, 64], P(('tp', 'grp')), may hold values from -0.03125 to 0.03125
- adapter_second_factor: bfloat16 [16, 64, 8192], P(('tp', 'grp')), may hold values from -0.75 to 0.75
Outputs:
- output: bfloat16 [1024, 8192], P(('rep', 'grp'), 'tp'), parts along dimension 0
The draws below stay inside these ranges and needn't reach their ends.
There are 2 independent parts, one for each index of `rep`. The reference program is written for one: setup_inputs(seed, part) draws one part's arguments, and reference() takes and returns one part's arrays. A program takes and returns all parts, laid end to end along the dimension named above; an argument that names none is the same for every part. Nothing has to cross between parts.
Inputs may be any that keep to these rules, and one draw needn't show every extreme that they name: `row_adapter_index`: in each row group (aligned blocks of 256 rows) no adapter is named by more than 64 rows, a bound that some block reaches.
All inputs are finite; a program needn't handle non-finite values.
Results may differ from the reference program's by a relative error of at most 0.0043.
Values may be sent and summed in bfloat16 or wider, within the bound.
No kernel may reach another device: no remote copies, remote signals or barrier semaphores. Data moves between devices by JAX's collectives and lax.ppermute only.
A program may use at most 192 MiB of HBM per device.

```python
import math
import jax
import jax.numpy as jnp
import numpy as np
from jax import lax

MODEL_DIM = 8192
HIDDEN_UNITS = 28672
ADAPTER_RANK = 64
ROWS = 256
ADAPTER_COUNT = 16
CAP = 64
TOTAL_ROWS = 512


def spiked(values, key, source, target, blocks, factor):
    owner, partner = [(jnp.arange(values.shape[axis_at]) // (values.shape[axis_at] // blocks)).reshape([-1 if axis == axis_at else 1 for axis in range(values.ndim)]) for axis_at in (source, target)]
    chosen = jax.random.permutation(key, blocks)[partner]
    strong = (owner == chosen) | (owner == (partner + blocks // 2) % blocks)
    return jnp.where(strong, factor * values, values)


def levels(stream_key, shape, cuts, least, top_value):
    def one(dim, blocks):
        draws = jax.random.uniform(jax.random.fold_in(jax.random.fold_in(stream_key, 6), dim), (blocks,), jnp.float32, least / len(cuts), top_value / len(cuts))
        return jnp.repeat(jnp.exp(draws), shape[dim] // blocks).reshape((-1,) + (1,) * (len(shape) - dim - 1))

    gain = one(*cuts[0])
    for cut in cuts[1:]:
        gain = gain * one(*cut)
    return gain


def deal_out(key, own, number, rows, count, top, most, slope):
    order = jax.random.permutation(key, count)
    packed, usual = shares(count, rows * top, most, slope, True), shares(count, rows * top, most, slope, False)
    places = jnp.arange(count)

    def named(lengths, turn):
        used = int((lengths > 0).sum())
        fixed = max(1, used // 4)
        passed = fixed + (places - fixed + turn * (used - fixed)) % max(1, count - fixed)
        return jnp.zeros((count,), jnp.int32).at[order[jnp.where(places < fixed, places, passed)]].set(jnp.asarray(lengths, jnp.int32))

    lengths = jnp.where(number % 4 == 0, named(packed, number // 4), named(usual, number - number // 4 - 1))
    mixed = jax.random.permutation(jax.random.fold_in(own, 3), count)
    donor, sink = mixed[0:count // 2 * 2:2], mixed[1:count // 2 * 2:2]
    room = jnp.minimum(lengths[donor] - 1, most - lengths[sink]) // 2
    room = jnp.where((donor == order[0]) | (sink == order[0]) | (lengths[sink] == 0), 0, jnp.maximum(room, 0))
    passed = jax.random.randint(jax.random.fold_in(own, 4), (count // 2,), 0, 1 << 20) % (room + 1)
    lengths = lengths.at[donor].add(-passed).at[sink].add(passed)
    labels = jnp.searchsorted(jnp.cumsum(lengths), jnp.arange(rows * top), side="right").astype(jnp.int32)
    listing = labels.reshape(top, rows).T
    listing = listing[jax.random.permutation(jax.random.fold_in(own, 1), rows)]
    turn = jax.random.randint(jax.random.fold_in(own, 2), (rows, 1), 0, top)
    return jnp.take_along_axis(listing, (jnp.arange(top)[None, :] + turn) % top, axis=1)


def shares(count, total, bound, skew, full):
    weights = [(1 << 20) // math.isqrt(rank ** skew) + 1 for rank in range(1, count + 1)]
    largest = bound if full else min(bound, max(-(-total // count), total * weights[0] // sum(weights)))
    least = 1 if total - largest >= count - 1 else 0
    given, spare = [largest] + [least] * (count - 1), total - largest - least * (count - 1)
    while spare > 0:
        movable = [i for i in range(1, count) if given[i] < largest] or [i for i in range(1, count) if given[i] < bound]
        pool, left = sum([weights[i] for i in movable]), spare
        for i in movable:
            extra = min(bound - given[i], max(1, left * weights[i] // pool), spare)
            given[i] = given[i] + extra
            spare = spare - extra
    return np.array(given)


def scatter_about(rng, shape, spread, bound, cuts=(), held_as=jnp.bfloat16):
    drawn = jax.random.normal(rng, shape, jnp.float32) * spread
    if len(cuts) > 0:
        drawn = levels(rng, shape, cuts, -0.22, 0.18) * drawn
    return jnp.clip(drawn, min=-bound, max=bound).astype(held_as)


def gaussian_with(stream_key, extent, deviation, bound, split, heavy, held_as=jnp.bfloat16):
    drawn = deviation * jax.random.normal(stream_key, extent, jnp.float32)
    if split:
        drawn = drawn * levels(stream_key, extent, split, -0.22, 0.18)
    return jnp.clip(spiked(drawn, jax.random.fold_in(stream_key, 3), *heavy), -bound, bound).astype(held_as)


def setup_inputs(seed: int = 0, part: int = 0) -> dict:
    splits = jax.random.split(jax.random.key(seed), 6)
    own_keys = jax.random.split(jax.random.fold_in(splits[5], part), 6)
    hidden = scatter_about(own_keys[0], (TOTAL_ROWS, HIDDEN_UNITS), 1.0, 6.0, ((0, 2), (1, 8)))
    row_adapter_index_keys = jax.random.split(jax.random.fold_in(own_keys[1], 1), TOTAL_ROWS // ROWS)
    row_adapter_index_turns = jax.random.permutation(jax.random.fold_in(own_keys[1], 3), TOTAL_ROWS // ROWS)
    row_adapter_index = jax.vmap(lambda own, number: deal_out(jax.random.fold_in(own_keys[1], 2), own, number, ROWS, ADAPTER_COUNT, 1, CAP, 2))(row_adapter_index_keys, row_adapter_index_turns).reshape((TOTAL_ROWS, 1))
    down_projection_weight = gaussian_with(splits[2], (HIDDEN_UNITS, MODEL_DIM), HIDDEN_UNITS ** -0.5, 0.046875, ((0, 8),), (0, 1, 8, 2.0))
    adapter_first_factor = scatter_about(splits[3], (ADAPTER_COUNT, HIDDEN_UNITS, ADAPTER_RANK), HIDDEN_UNITS ** -0.5, 0.03125, ((0, 16),))
    adapter_second_factor = scatter_about(splits[4], (ADAPTER_COUNT, ADAPTER_RANK, MODEL_DIM), ADAPTER_RANK ** -0.5, 0.75, ((0, 16),))
    return dict(hidden=hidden, row_adapter_index=row_adapter_index, down_projection_weight=down_projection_weight, adapter_first_factor=adapter_first_factor, adapter_second_factor=adapter_second_factor)


def reference(hidden, row_adapter_index, down_projection_weight, adapter_first_factor, adapter_second_factor):
    base_sum = jnp.dot(hidden, down_projection_weight, preferred_element_type=jnp.float32)

    def one_row(pair):
        hidden_activation_row, row_ident = pair
        adapter_choice = row_ident[0].astype(jnp.int32)
        adapter_latent = jnp.dot(hidden_activation_row[None, :], adapter_first_factor[adapter_choice], preferred_element_type=jnp.float32).astype(jnp.bfloat16)
        adapter_row_update = jnp.dot(adapter_latent, adapter_second_factor[adapter_choice], preferred_element_type=jnp.float32).astype(jnp.bfloat16)
        return adapter_row_update[0]

    adapter_row_update = lax.map(one_row, (hidden, row_adapter_index))
    return (base_sum + adapter_row_update.astype(jnp.float32)).astype(jnp.bfloat16)
```

```python
import jax
import jax.numpy as jnp
from jax import lax
from jax.experimental import pallas as pl
from jax.experimental.pallas import tpu as pltpu
from jax.sharding import PartitionSpec as P

SWAP = ((0, 1), (1, 0))


def block_products(hidden, weight, block_ids, block_count, block_columns, out_dtype):
    rows, depth = hidden.shape

    def kernel(ids_ref, hidden_ref, weight_ref, out_ref):
        out_ref[0] = jnp.dot(
            hidden_ref[...], weight_ref[...], preferred_element_type=jnp.float32
        ).astype(out_dtype)

    return pl.pallas_call(
        kernel,
        out_shape=jax.ShapeDtypeStruct((block_count, rows, block_columns), out_dtype),
        grid_spec=pltpu.PrefetchScalarGridSpec(
            num_scalar_prefetch=1,
            grid=(block_count,),
            in_specs=[
                pl.BlockSpec((rows, depth), lambda b, ids: (0, 0)),
                pl.BlockSpec((depth, block_columns), lambda b, ids: (0, ids[b])),
            ],
            out_specs=pl.BlockSpec((1, rows, block_columns), lambda b, ids: (b, 0, 0)),
        ),
        compiler_params=pltpu.CompilerParams(vmem_limit_bytes=40 * 2**20),
        cost_estimate=pl.CostEstimate(
            flops=2 * rows * depth * block_columns * block_count,
            bytes_accessed=2 * depth * block_columns * block_count,
            transcendentals=0,
        ),
    )(block_ids, hidden, weight)


def local(
    hidden, row_adapter_index, down_projection_weight, adapter_first_factor, adapter_second_factor
):
    tp = lax.axis_size("tp")
    t = lax.axis_index("tp")
    y = lax.axis_index("rep")
    g = lax.axis_index("grp")
    rows, depth = hidden.shape
    rank = adapter_first_factor.shape[2]
    columns = down_projection_weight.shape[1] // tp
    half = depth // 2
    lanes = 2 * rank

    first = adapter_first_factor[0].T.reshape(rank, tp, 2, half)
    first = lax.dynamic_index_in_dim(first, y, 2, keepdims=False).transpose(1, 0, 2)
    first = lax.all_to_all(first, "tp", split_axis=0, concat_axis=0, tiled=True)
    first = first.reshape(tp * rank, half)

    tag = jnp.broadcast_to(row_adapter_index.astype(jnp.bfloat16), (rows, 128))

    def piece(which):
        return jnp.concatenate(
            [lax.dynamic_slice(hidden, (0, which * half), (rows, half)), tag], axis=1
        )

    mine = piece(y)
    from_rep = lax.ppermute(piece(1 - y), "rep", SWAP)
    pair = jnp.concatenate([mine, from_rep], axis=0)
    from_grp = lax.ppermute(pair, "grp", SWAP)

    def latents(block):
        full = lax.dot_general(
            block[:, :half], first, (((1,), (1,)), ((), ())), preferred_element_type=jnp.float32
        )
        adapter = block[:, half:].astype(jnp.int32)
        place = lax.broadcasted_iota(jnp.int32, (block.shape[0], lanes), 1) // rank
        adapter = adapter[:, :lanes]
        total = jnp.zeros((block.shape[0], lanes), jnp.float32)
        for two in range(tp // 2):
            total += jnp.where(
                adapter == (2 * two + place) * 2 + g, full[:, two * lanes : (two + 1) * lanes], 0.0
            )
        return total

    near = latents(pair)
    far = latents(from_grp)
    to_rep = jnp.stack([near[rows:], far[rows:]])
    got = lax.ppermute(to_rep, "rep", SWAP)
    latent = near[:rows] + got[0]
    latent = latent + lax.ppermute(far[:rows] + got[1], "grp", SWAP)
    step = 1
    while step < tp:
        latent = latent + lax.ppermute(latent, "tp", [(i, i ^ step) for i in range(tp)])
        step *= 2
    latent = latent.astype(jnp.bfloat16)

    second = adapter_second_factor[0].reshape(rank, tp, 2, columns // 2)
    second = lax.dynamic_index_in_dim(second, y, 2, keepdims=False).transpose(1, 0, 2)
    second = lax.all_to_all(second, "tp", split_axis=0, concat_axis=0, tiled=True)
    second = second.reshape(tp * rank, columns // 2)
    other = lax.ppermute(second, "rep", SWAP)
    second = jnp.where(
        y == 0,
        jnp.concatenate([second, other], axis=1),
        jnp.concatenate([other, second], axis=1),
    )
    second_twin = lax.ppermute(second, "grp", SWAP)

    place = lax.broadcasted_iota(jnp.int32, (rows, tp * rank), 1) // rank
    wide = jnp.tile(latent, (1, tp // 2))
    zero = jnp.zeros((), jnp.bfloat16)
    delta = jnp.dot(
        jnp.where(row_adapter_index == place * 2 + g, wide, zero),
        second,
        preferred_element_type=jnp.float32,
    ) + jnp.dot(
        jnp.where(row_adapter_index == place * 2 + 1 - g, wide, zero),
        second_twin,
        preferred_element_type=jnp.float32,
    )

    part = {}
    for j in range(tp - 1, 0, -2):
        part[j] = block_products(
            hidden, down_projection_weight, (t ^ j).reshape(1), 1, columns, jnp.bfloat16
        )[0]
    kept = list(range(tp - 2, -1, -2))
    products = block_products(
        hidden,
        down_projection_weight,
        jnp.stack([t ^ j for j in kept]),
        len(kept),
        columns,
        jnp.float32,
    )
    for i, j in enumerate(kept):
        part[j] = products[i]
    step = 1
    while step < tp:
        for j in range(tp - step, 0, -2 * step):
            sent = lax.ppermute(
                part[j].astype(jnp.bfloat16), "tp", [(i, i ^ step) for i in range(tp)]
            )
            part[j ^ step] = part[j ^ step] + sent.astype(jnp.float32)
        step *= 2
    return (part[0] + delta.astype(jnp.bfloat16).astype(jnp.float32)).astype(jnp.bfloat16)


def solution(mesh):
    return jax.shard_map(
        local,
        mesh=mesh,
        in_specs=(
            P(("rep", "grp"), "tp"),
            P(("rep", "grp"), None),
            P("tp", None),
            P(("tp", "grp"), None, None),
            P(("tp", "grp"), None, None),
        ),
        out_specs=P(("rep", "grp"), "tp"),
        check_vma=False,
    )
```

```python
import jax
import jax.numpy as jnp
from jax import lax
from jax.experimental import pallas as pl
from jax.experimental.pallas import tpu as pltpu
from jax.sharding import PartitionSpec as P

SWAP = ((0, 1), (1, 0))
ANY = pl.BlockSpec(memory_space=pl.ANY)
VMEM = pl.BlockSpec(memory_space=pltpu.VMEM)
TAG_ROWS = 16


def params():
    return pltpu.CompilerParams(vmem_limit_bytes=48 * 2**20)


def block_products(hidden, weight, block_ids, block_columns, out_dtype, after):
    rows, depth = hidden.shape
    count = len(block_ids)

    def kernel(ids_ref, hidden_ref, weight_ref, after_ref, *out_refs):
        for i, out_ref in enumerate(out_refs):

            @pl.when(pl.program_id(0) == i)
            def _():
                out_ref[...] = jnp.dot(
                    hidden_ref[...], weight_ref[...], preferred_element_type=jnp.float32
                ).astype(out_dtype)

    return pl.pallas_call(
        kernel,
        out_shape=[jax.ShapeDtypeStruct((rows, block_columns), out_dtype)] * count,
        grid_spec=pltpu.PrefetchScalarGridSpec(
            num_scalar_prefetch=1,
            grid=(count,),
            in_specs=[
                pl.BlockSpec((rows, depth), lambda b, ids: (0, 0)),
                pl.BlockSpec((depth, block_columns), lambda b, ids: (0, ids[b])),
                ANY,
            ],
            out_specs=[pl.BlockSpec((rows, block_columns), lambda b, ids: (0, 0))] * count,
        ),
        compiler_params=params(),
        cost_estimate=pl.CostEstimate(
            flops=2 * rows * depth * block_columns * count,
            bytes_accessed=2 * depth * block_columns * count,
            transcendentals=0,
        ),
    )(jnp.stack(block_ids), hidden, weight, after)


def pack_columns(source, pieces, width, y, after):
    rows = source.shape[0]
    if width % 128:
        parts = source.reshape(rows, pieces, 2, width)
        return lax.dynamic_index_in_dim(parts, y, 2, keepdims=False).transpose(1, 0, 2)

    def kernel(y_ref, source_ref, after_ref, out_ref, buffer, in_sem, out_sem):
        def fetch(i):
            start = pl.multiple_of((2 * i + y_ref[0]) * width, 128)
            return pltpu.make_async_copy(
                source_ref.at[:, pl.ds(start, width)], buffer.at[i], in_sem.at[i]
            )

        def store(i):
            return pltpu.make_async_copy(buffer.at[i], out_ref.at[i], out_sem.at[i])

        for i in range(pieces):
            fetch(i).start()
        for i in range(pieces):
            fetch(i).wait()
            store(i).start()
        for i in range(pieces):
            store(i).wait()

    return pl.pallas_call(
        kernel,
        out_shape=jax.ShapeDtypeStruct((pieces, rows, width), source.dtype),
        in_specs=[pl.BlockSpec(memory_space=pltpu.SMEM), ANY, ANY],
        out_specs=ANY,
        scratch_shapes=[
            pltpu.VMEM((pieces, rows, width), source.dtype),
            pltpu.SemaphoreType.DMA((pieces,)),
            pltpu.SemaphoreType.DMA((pieces,)),
        ],
        compiler_params=params(),
        cost_estimate=pl.CostEstimate(
            flops=0, bytes_accessed=4 * pieces * rows * width, transcendentals=0
        ),
    )(y.reshape(1), source, after)


def pack_hidden(hidden, tags, half, y, after):
    rows = hidden.shape[0]
    if half % 128 or half < rows:
        return [
            jnp.concatenate(
                [lax.dynamic_slice(hidden, (0, which * half), (rows, half)), tags], axis=0
            )
            for which in (y, 1 - y)
        ]
    chunks = 4
    step = rows // chunks

    def kernel(y_ref, hidden_ref, tags_ref, after_ref, mine_ref, other_ref, buffer, in_sem, out_sem):
        def fetch(which, i):
            half_index = y_ref[0] if which == 0 else 1 - y_ref[0]
            return pltpu.make_async_copy(
                hidden_ref.at[
                    pl.ds(i * step, step), pl.ds(pl.multiple_of(half_index * half, 128), half)
                ],
                buffer.at[which, pl.ds(i * step, step)],
                in_sem.at[which, i],
            )

        def store(which):
            out_ref = (mine_ref, other_ref)[which]
            return pltpu.make_async_copy(buffer.at[which], out_ref, out_sem.at[which])

        for which in (1, 0):
            for i in range(chunks):
                fetch(which, i).start()
        for which in (1, 0):
            buffer[which, rows:] = tags_ref[...]
        for which in (1, 0):
            for i in range(chunks):
                fetch(which, i).wait()
            store(which).start()
        for which in (1, 0):
            store(which).wait()

    shape = jax.ShapeDtypeStruct((rows + TAG_ROWS, half), hidden.dtype)
    return pl.pallas_call(
        kernel,
        out_shape=[shape, shape],
        in_specs=[pl.BlockSpec(memory_space=pltpu.SMEM), ANY, VMEM, ANY],
        out_specs=[ANY, ANY],
        scratch_shapes=[
            pltpu.VMEM((2, rows + TAG_ROWS, half), hidden.dtype),
            pltpu.SemaphoreType.DMA((2, chunks)),
            pltpu.SemaphoreType.DMA((2,)),
        ],
        compiler_params=params(),
        cost_estimate=pl.CostEstimate(
            flops=0, bytes_accessed=8 * rows * half, transcendentals=0
        ),
    )(y.reshape(1), hidden, tags, after)


def latent_terms(first, blocks, rows, rank, g, after):
    count, half = first.shape
    tp = count // rank

    def term(factor, rows_held, adapter, core):
        full = lax.dot_general(
            factor, rows_held, (((1,), (1,)), ((), ())), preferred_element_type=jnp.float32
        )
        total = jnp.zeros((rank, rows), jnp.float32)
        for place in range(tp):
            total += jnp.where(
                adapter == place * 2 + core, full[place * rank : (place + 1) * rank], 0.0
            )
        return total

    if half % 128 or half < rows:
        return [
            term(
                first, block[:rows], block[rows:].reshape(-1)[:rows][None].astype(jnp.int32), g
            )
            for block in blocks
        ]

    def kernel(g_ref, first_ref, *refs):
        block_refs, out_refs = refs[: len(blocks)], refs[len(blocks) + 1 :]
        for block_ref, out_ref in zip(block_refs, out_refs):
            tag = block_ref[rows:, :rows].astype(jnp.float32)[0:1].astype(jnp.int32)
            out_ref[...] = term(first_ref[...], block_ref[:rows, :], tag, g_ref[0])

    return pl.pallas_call(
        kernel,
        out_shape=[jax.ShapeDtypeStruct((rank, rows), jnp.float32)] * len(blocks),
        in_specs=[pl.BlockSpec(memory_space=pltpu.SMEM), VMEM] + [VMEM] * len(blocks) + [ANY],
        out_specs=[VMEM] * len(blocks),
        compiler_params=params(),
        cost_estimate=pl.CostEstimate(
            flops=2 * count * half * rows * len(blocks),
            bytes_accessed=2 * half * (count + rows * len(blocks)),
            transcendentals=0,
        ),
    )(g.reshape(1), first, *blocks, after)


def finish(latent, adapter, seconds, base, received, y, g):
    rows, columns = base.shape
    rank = latent.shape[0]
    tp = seconds[0].shape[0] // rank
    half = columns // 2

    def spread(held, ids, core):
        zero = jnp.zeros_like(held)
        return jnp.concatenate(
            [jnp.where(ids == place * 2 + core, held, zero) for place in range(tp)], axis=0
        )

    def product(left, right):
        return lax.dot_general(
            left, right, (((0,), (0,)), ((), ())), preferred_element_type=jnp.float32
        )

    if half % 128:
        near = spread(latent, adapter, g).astype(jnp.bfloat16)
        far = spread(latent, adapter, 1 - g).astype(jnp.bfloat16)
        mine = product(near, seconds[0]) + product(far, seconds[2])
        other = product(near, seconds[1]) + product(far, seconds[3])
        delta = jnp.where(
            y == 0,
            jnp.concatenate([mine, other], axis=1),
            jnp.concatenate([other, mine], axis=1),
        )
        total = base
        for block in received:
            total = total + block.astype(jnp.float32)
        return (total + delta.astype(jnp.bfloat16).astype(jnp.float32)).astype(jnp.bfloat16)

    def kernel(y_ref, g_ref, latent_ref, adapter_ref, *refs):
        second_refs, base_ref, received_refs, out_ref = refs[:4], refs[4], refs[5:-1], refs[-1]
        held = latent_ref[...].astype(jnp.bfloat16).astype(jnp.float32)
        near = spread(held, adapter_ref[...], g_ref[0]).astype(jnp.bfloat16)
        far = spread(held, adapter_ref[...], 1 - g_ref[0]).astype(jnp.bfloat16)
        for which in range(2):
            index = y_ref[0] if which == 0 else 1 - y_ref[0]
            lanes = pl.ds(pl.multiple_of(index * half, 128), half)
            delta = product(near, second_refs[which][...])
            delta += product(far, second_refs[2 + which][...])
            total = base_ref[:, lanes]
            for received_ref in received_refs:
                total += received_ref[:, lanes].astype(jnp.float32)
            total += delta.astype(jnp.bfloat16).astype(jnp.float32)
            out_ref[:, lanes] = total.astype(jnp.bfloat16)

    smem = pl.BlockSpec(memory_space=pltpu.SMEM)
    return pl.pallas_call(
        kernel,
        out_shape=jax.ShapeDtypeStruct((rows, columns), jnp.bfloat16),
        in_specs=[smem, smem] + [VMEM] * (7 + len(received)),
        out_specs=VMEM,
        compiler_params=params(),
        cost_estimate=pl.CostEstimate(
            flops=4 * tp * rank * rows * columns,
            bytes_accessed=rows * columns * (6 + 2 * len(received)) + 4 * tp * rank * columns,
            transcendentals=0,
        ),
    )(y.reshape(1), g.reshape(1), latent, adapter, *seconds, base, *received)


def local(
    hidden, row_adapter_index, down_projection_weight, adapter_first_factor, adapter_second_factor
):
    tp = lax.axis_size("tp")
    t = lax.axis_index("tp")
    y = lax.axis_index("rep")
    g = lax.axis_index("grp")
    rows, depth = hidden.shape
    rank = adapter_first_factor.shape[2]
    columns = down_projection_weight.shape[1] // tp
    half = depth // 2
    adapter = row_adapter_index.T

    def across(step):
        return [(i, i ^ step) for i in range(tp)]

    first = pack_columns(adapter_first_factor[0].T, tp, half, y, row_adapter_index)
    packed_first = first
    first = lax.all_to_all(first, "tp", split_axis=0, concat_axis=0, tiled=True)
    first = first.reshape(tp * rank, half)

    part = {}

    def multiply(js, out_dtype, after):
        outs = block_products(
            hidden, down_projection_weight, [t ^ j for j in js], columns, out_dtype, after
        )
        part.update(zip(js, outs))
        return outs[-1]

    odd = list(range(tp - 1, 0, -2))
    even = [j - 1 for j in odd]
    last = multiply(odd[:1], jnp.bfloat16, packed_first)

    tag_lanes = jnp.pad(adapter[0], (0, -rows % half if rows > half else half - rows))
    tags = tag_lanes.astype(jnp.bfloat16).reshape(-1, half)
    tags = jnp.pad(tags, ((0, TAG_ROWS - tags.shape[0]), (0, 0)))
    mine, other = pack_hidden(hidden, tags, half, y, last)
    from_rep = lax.ppermute(other, "rep", SWAP)
    from_grp = lax.ppermute(mine, "grp", SWAP)

    last = multiply(odd[1:3], jnp.bfloat16, mine)
    if odd[3:]:
        last = multiply(odd[3:], jnp.bfloat16, last)
    second = pack_columns(adapter_second_factor[0], tp, columns // 2, y, last)
    last = multiply(even, jnp.float32, second)
    second = lax.all_to_all(second, "tp", split_axis=0, concat_axis=0, tiled=True)
    second = second.reshape(tp * rank, columns // 2)
    second_other = lax.ppermute(second, "rep", SWAP)
    seconds = [
        second,
        second_other,
        lax.ppermute(second, "grp", SWAP),
        lax.ppermute(second_other, "grp", SWAP),
    ]

    from_both = lax.ppermute(from_rep, "grp", SWAP)
    away = latent_terms(first, [from_rep, from_both], rows, rank, g, last)
    here = latent_terms(first, [mine, from_grp], rows, rank, g, away[0])
    got = lax.ppermute(jnp.stack(away), "rep", SWAP)
    latent = here[0] + got[0] + lax.ppermute(here[1] + got[1], "grp", SWAP)
    step = 1
    while step < tp:
        latent = latent + lax.ppermute(latent, "tp", across(step))
        step *= 2
    latent = latent.astype(jnp.bfloat16).astype(jnp.float32)

    received = []
    step = 1
    while step < tp:
        for j in range(tp - step, 0, -2 * step):
            sent = lax.ppermute(part[j].astype(jnp.bfloat16), "tp", across(step))
            if j == step:
                received.append(sent)
            else:
                part[j ^ step] = part[j ^ step] + sent.astype(jnp.float32)
        step *= 2
    return finish(latent, adapter, seconds, part[0], received, y, g)


def solution(mesh):
    return jax.shard_map(
        local,
        mesh=mesh,
        in_specs=(
            P(("rep", "grp"), "tp"),
            P(("rep", "grp"), None),
            P("tp", None),
            P(("tp", "grp"), None, None),
            P(("tp", "grp"), None, None),
        ),
        out_specs=P(("rep", "grp"), "tp"),
        check_vma=False,
    )
```

```python
import jax
import jax.numpy as jnp
from jax import lax
from jax.experimental import pallas as pl
from jax.experimental.pallas import tpu as pltpu
from jax.sharding import PartitionSpec as P

SWAP = ((0, 1), (1, 0))
ANY = pl.BlockSpec(memory_space=pl.ANY)
VMEM = pl.BlockSpec(memory_space=pltpu.VMEM)
SMEM = pl.BlockSpec(memory_space=pltpu.SMEM)
TAG_ROWS = 16
COST = pl.CostEstimate(flops=1, bytes_accessed=1, transcendentals=0)
PARAMS = pltpu.CompilerParams(vmem_limit_bytes=64 * 2**20)


class Order:
    def __init__(self, array):
        self.last = array


def relay(array, order):
    def kernel(array_ref, after_ref, out_ref):
        del array_ref, after_ref, out_ref

    out = pl.pallas_call(
        kernel,
        out_shape=jax.ShapeDtypeStruct(array.shape, array.dtype),
        in_specs=[ANY, ANY],
        out_specs=ANY,
        input_output_aliases={0: 0},
        compiler_params=PARAMS,
        cost_estimate=COST,
    )(array, order.last)
    order.last = out
    return out


def block_products(hidden, weight, sent_ids, kept_ids, columns, order):
    rows, depth = hidden.shape
    sent, kept = len(sent_ids), len(kept_ids)

    def kernel(ids_ref, hidden_ref, weight_ref, after_ref, *out_refs):
        product = jnp.dot(hidden_ref[...], weight_ref[...], preferred_element_type=jnp.float32)
        if sent:

            @pl.when(pl.program_id(0) < sent)
            def _():
                out_refs[0][0] = product.astype(jnp.bfloat16)

        if kept:

            @pl.when(pl.program_id(0) >= sent)
            def _():
                out_refs[-1][0] = product

    out_shape, out_specs = [], []
    if sent:
        out_shape.append(jax.ShapeDtypeStruct((sent, rows, columns), jnp.bfloat16))
        out_specs.append(
            pl.BlockSpec((1, rows, columns), lambda b, ids: (jnp.minimum(b, sent - 1), 0, 0))
        )
    if kept:
        out_shape.append(jax.ShapeDtypeStruct((kept, rows, columns), jnp.float32))
        out_specs.append(
            pl.BlockSpec((1, rows, columns), lambda b, ids: (jnp.maximum(b - sent, 0), 0, 0))
        )
    outs = pl.pallas_call(
        kernel,
        out_shape=out_shape,
        grid_spec=pltpu.PrefetchScalarGridSpec(
            num_scalar_prefetch=1,
            grid=(sent + kept,),
            in_specs=[
                pl.BlockSpec((rows, depth), lambda b, ids: (0, 0)),
                pl.BlockSpec((depth, columns), lambda b, ids: (0, ids[b])),
                ANY,
            ],
            out_specs=out_specs,
        ),
        compiler_params=PARAMS,
        cost_estimate=COST,
    )(jnp.stack(sent_ids + kept_ids), hidden, weight, order.last)
    order.last = outs[-1]
    return outs


def pack_factors(first, second, tp, y):
    rank = first.shape[0]
    widths = [first.shape[1] // (2 * tp), second.shape[1] // (2 * tp)]
    if widths[0] % 128 or widths[1] % 128:
        parts = [
            lax.dynamic_index_in_dim(
                source.reshape(rank, tp, 2, width), y, 2, keepdims=False
            ).transpose(1, 0, 2)
            for source, width in zip((first, second), widths)
        ]
        return jnp.concatenate(parts, axis=2)
    places = [pl.ds(0, widths[0]), pl.ds(widths[0], widths[1])]

    def kernel(y_ref, first_ref, second_ref, out_ref, buffer, in_sem, out_sem):
        def fetch(i, which):
            width = widths[which]
            start = pl.multiple_of((2 * i + y_ref[0]) * width, 128)
            return pltpu.make_async_copy(
                (first_ref, second_ref)[which].at[:, pl.ds(start, width)],
                buffer.at[i, :, places[which]],
                in_sem.at[i, which],
            )

        def store(i):
            return pltpu.make_async_copy(buffer.at[i], out_ref.at[i], out_sem.at[i])

        for i in range(tp):
            for which in range(2):
                fetch(i, which).start()
        for i in range(tp):
            for which in range(2):
                fetch(i, which).wait()
            store(i).start()
        for i in range(tp):
            store(i).wait()

    shape = (tp, rank, sum(widths))
    return pl.pallas_call(
        kernel,
        out_shape=jax.ShapeDtypeStruct(shape, first.dtype),
        in_specs=[SMEM, ANY, ANY],
        out_specs=ANY,
        scratch_shapes=[
            pltpu.VMEM(shape, first.dtype),
            pltpu.SemaphoreType.DMA((tp, 2)),
            pltpu.SemaphoreType.DMA((tp,)),
        ],
        compiler_params=PARAMS,
        cost_estimate=COST,
    )(y.reshape(1), first, second)


def pack_hidden(hidden, tags, half, y, order):
    rows = hidden.shape[0]
    if half % 128 or half < rows:
        return [
            jnp.concatenate(
                [lax.dynamic_slice(hidden, (0, which * half), (rows, half)), tags], axis=0
            )
            for which in (y, 1 - y)
        ]
    chunks = 4
    step = rows // chunks

    def kernel(y_ref, hidden_ref, tags_ref, after_ref, mine_ref, other_ref, buffer, in_sem, out_sem):
        def fetch(which, i):
            half_index = y_ref[0] if which == 0 else 1 - y_ref[0]
            return pltpu.make_async_copy(
                hidden_ref.at[
                    pl.ds(i * step, step), pl.ds(pl.multiple_of(half_index * half, 128), half)
                ],
                buffer.at[which, pl.ds(i * step, step)],
                in_sem.at[which, i],
            )

        def store(which):
            out_ref = (mine_ref, other_ref)[which]
            return pltpu.make_async_copy(buffer.at[which], out_ref, out_sem.at[which])

        for which in (1, 0):
            for i in range(chunks):
                fetch(which, i).start()
        for which in (1, 0):
            buffer[which, rows:] = tags_ref[...]
        for which in (1, 0):
            for i in range(chunks):
                fetch(which, i).wait()
            store(which).start()
        for which in (1, 0):
            store(which).wait()

    shape = jax.ShapeDtypeStruct((rows + TAG_ROWS, half), hidden.dtype)
    mine, other = pl.pallas_call(
        kernel,
        out_shape=[shape, shape],
        in_specs=[SMEM, ANY, VMEM, ANY],
        out_specs=[ANY, ANY],
        scratch_shapes=[
            pltpu.VMEM((2, rows + TAG_ROWS, half), hidden.dtype),
            pltpu.SemaphoreType.DMA((2, chunks)),
            pltpu.SemaphoreType.DMA((2,)),
        ],
        compiler_params=PARAMS,
        cost_estimate=COST,
    )(y.reshape(1), hidden, tags, order.last)
    order.last = mine
    return mine, other


def latent_terms(factors, half, blocks, rows, rank, g, with_second, order):
    count = factors.shape[0]
    tp = count // rank

    def term(factor, rows_held, adapter, core):
        full = lax.dot_general(
            factor, rows_held, (((1,), (1,)), ((), ())), preferred_element_type=jnp.float32
        )
        total = jnp.zeros((rank, rows), jnp.float32)
        for place in range(tp):
            total += jnp.where(
                adapter == place * 2 + core, full[place * rank : (place + 1) * rank], 0.0
            )
        return total

    if half % 128 or half < rows:
        outs = [
            term(
                factors[:, :half],
                block[:rows],
                block[rows:].reshape(-1)[:rows][None].astype(jnp.int32),
                g,
            )
            for block in blocks
        ]
        return [jnp.stack(outs)] + [factors[:, half:]] * with_second

    def kernel(g_ref, factors_ref, *refs):
        block_refs, out_refs = refs[: len(blocks)], refs[len(blocks) + 1 :]
        for i, block_ref in enumerate(block_refs):
            tag = block_ref[rows:, :rows].astype(jnp.float32)[0:1].astype(jnp.int32)
            out_refs[0][i] = term(factors_ref[:, :half], block_ref[:rows, :], tag, g_ref[0])
        if with_second:
            out_refs[-1][...] = factors_ref[:, half:]

    out_shape = [jax.ShapeDtypeStruct((len(blocks), rank, rows), jnp.float32)]
    if with_second:
        out_shape.append(jax.ShapeDtypeStruct((count, factors.shape[1] - half), factors.dtype))
    outs = pl.pallas_call(
        kernel,
        out_shape=out_shape,
        in_specs=[SMEM, VMEM] + [VMEM] * len(blocks) + [ANY],
        out_specs=[VMEM] * len(out_shape),
        compiler_params=PARAMS,
        cost_estimate=COST,
    )(g.reshape(1), factors, *blocks, order.last)
    order.last = outs[0]
    return outs


def block_specs(blocks):
    return [
        pl.BlockSpec((1, *array.shape[1:]), lambda b, i=i: (i, 0, 0)) for array, i in blocks
    ]


def add(pairs, order):
    blocks = [block for pair in pairs for block in pair]
    shape = blocks[0][0].shape[1:]

    def kernel(*refs):
        outs = refs[len(blocks) + 1 :]
        for i, out_ref in enumerate(outs):
            out_ref[...] = refs[2 * i][...] + refs[2 * i + 1][...]

    outs = pl.pallas_call(
        kernel,
        grid=(1,),
        out_shape=[jax.ShapeDtypeStruct((1, *shape), jnp.float32)] * len(pairs),
        in_specs=block_specs(blocks) + [ANY],
        out_specs=[pl.BlockSpec((1, *shape), lambda b: (0, 0, 0))] * len(pairs),
        compiler_params=PARAMS,
        cost_estimate=COST,
    )(*[array for array, _ in blocks], order.last)
    order.last = outs[0]
    return outs


def fold(blocks, dtype, order):
    shape = blocks[0][0].shape[1:]

    def kernel(*refs):
        total = refs[0][0]
        for ref in refs[1 : len(blocks)]:
            total += ref[0].astype(jnp.float32)
        refs[-1][0] = total.astype(dtype)

    out = pl.pallas_call(
        kernel,
        grid=(1,),
        out_shape=jax.ShapeDtypeStruct((1, *shape), dtype),
        in_specs=block_specs(blocks) + [ANY],
        out_specs=pl.BlockSpec((1, *shape), lambda b: (0, 0, 0)),
        compiler_params=PARAMS,
        cost_estimate=COST,
    )(*[array for array, _ in blocks], order.last)
    order.last = out
    return out


def finish(latents, adapter, seconds, blocks, y, g):
    rows, columns = blocks[0][0].shape[1:]
    rank = latents[0].shape[1]
    tp = seconds[0].shape[0] // rank
    half = columns // 2

    def spread(held, ids, core):
        zero = jnp.zeros_like(held)
        return jnp.concatenate(
            [jnp.where(ids == place * 2 + core, held, zero) for place in range(tp)], axis=0
        ).astype(jnp.bfloat16)

    def product(left, right):
        return lax.dot_general(
            left, right, (((0,), (0,)), ((), ())), preferred_element_type=jnp.float32
        )

    if half % 128:
        latent = (latents[0][0] + latents[1][0]).astype(jnp.bfloat16).astype(jnp.float32)
        near, far = spread(latent, adapter, g), spread(latent, adapter, 1 - g)
        mine = product(near, seconds[0]) + product(far, seconds[2])
        other = product(near, seconds[1]) + product(far, seconds[3])
        delta = jnp.where(
            y == 0,
            jnp.concatenate([mine, other], axis=1),
            jnp.concatenate([other, mine], axis=1),
        )
        total = delta.astype(jnp.bfloat16).astype(jnp.float32)
        for array, i in blocks:
            total = total + array[i].astype(jnp.float32)
        return total.astype(jnp.bfloat16)

    def kernel(y_ref, g_ref, a_ref, b_ref, adapter_ref, *refs):
        second_refs, block_refs, out_ref = refs[:4], refs[4:-1], refs[-1]
        latent = (a_ref[0] + b_ref[0]).astype(jnp.bfloat16).astype(jnp.float32)
        near = spread(latent, adapter_ref[...], g_ref[0])
        far = spread(latent, adapter_ref[...], 1 - g_ref[0])
        for which in range(2):
            index = y_ref[0] if which == 0 else 1 - y_ref[0]
            lanes = pl.ds(pl.multiple_of(index * half, 128), half)
            delta = product(near, second_refs[which][...])
            delta += product(far, second_refs[2 + which][...])
            total = block_refs[0][0, :, lanes]
            for block_ref in block_refs[1:]:
                total += block_ref[0, :, lanes].astype(jnp.float32)
            total += delta.astype(jnp.bfloat16).astype(jnp.float32)
            out_ref[:, lanes] = total.astype(jnp.bfloat16)

    whole = lambda array: pl.BlockSpec(array.shape, lambda b: (0,) * array.ndim)
    return pl.pallas_call(
        kernel,
        grid=(1,),
        out_shape=jax.ShapeDtypeStruct((rows, columns), jnp.bfloat16),
        in_specs=[SMEM, SMEM]
        + [whole(array) for array in (*latents, adapter, *seconds)]
        + block_specs(blocks),
        out_specs=pl.BlockSpec((rows, columns), lambda b: (0, 0)),
        compiler_params=PARAMS,
        cost_estimate=COST,
    )(y.reshape(1), g.reshape(1), *latents, adapter, *seconds, *[array for array, _ in blocks])


def local(
    hidden, row_adapter_index, down_projection_weight, adapter_first_factor, adapter_second_factor
):
    tp = lax.axis_size("tp")
    t = lax.axis_index("tp")
    y = lax.axis_index("rep")
    g = lax.axis_index("grp")
    rows, depth = hidden.shape
    rank = adapter_first_factor.shape[2]
    columns = down_projection_weight.shape[1] // tp
    half = depth // 2
    adapter = row_adapter_index.T

    def across(array, step):
        return lax.ppermute(array, "tp", [(i, i ^ step) for i in range(tp)])

    factors = pack_factors(adapter_first_factor[0].T, adapter_second_factor[0], tp, y)
    order = Order(factors)
    factors = lax.all_to_all(factors, "tp", split_axis=0, concat_axis=0, tiled=True)
    factors = factors.reshape(tp * rank, factors.shape[2])

    terms = {j: [] for j in range(0, tp, 2)}

    def multiply(sent, kept):
        outs = block_products(
            hidden,
            down_projection_weight,
            [t ^ j for j in sent],
            [t ^ j for j in kept],
            columns,
            order,
        )
        for i, j in enumerate(kept):
            terms[j].insert(0, (outs[-1], i))
        if sent:
            got = across(outs[0], 1)
            for i, j in enumerate(sent):
                terms[j ^ 1].append((got, i))

    def pass_on(step, j):
        terms[j ^ step].append((across(fold(terms[j], jnp.bfloat16, order), step), 0))

    odd = list(range(tp - 1, 0, -2))
    even = [j - 1 for j in odd]
    stages = []
    step = 2
    while step < tp:
        stages.append([(step, j) for j in range(tp - step, 0, -2 * step)])
        step *= 2
    multiply(odd[:1], [])

    tag_lanes = jnp.pad(adapter[0], (0, -rows % half if rows > half else half - rows))
    tags = tag_lanes.astype(jnp.bfloat16).reshape(-1, half)
    tags = jnp.pad(tags, ((0, TAG_ROWS - tags.shape[0]), (0, 0)))
    mine, other = pack_hidden(hidden, tags, half, y, order)
    from_rep = lax.ppermute(other, "rep", SWAP)
    from_grp = lax.ppermute(mine, "grp", SWAP)

    multiply(odd[1:3], [])
    multiply(odd[3:], even[:1])
    from_rep = relay(from_rep, order)
    from_both = lax.ppermute(from_rep, "grp", SWAP)
    pass_on(*stages[0][0])
    multiply([], even[1:])
    for item in stages[0][1:]:
        pass_on(*item)

    away = latent_terms(factors, half, [from_rep, from_both], rows, rank, g, False, order)[0]
    got = lax.ppermute(away, "rep", SWAP)
    near, second = latent_terms(
        factors, half, [mine, from_grp], rows, rank, g, True, order
    )
    second_other = lax.ppermute(second, "rep", SWAP)
    early = list(terms[0])
    for stage in stages[1:]:
        for item in stage:
            pass_on(*item)
    terms[0] = [(fold(early, jnp.float32, order), 0)] + terms[0][len(early) :]
    here, there = add([((near, i), (got, i)) for i in range(2)], order)
    latents = [here, lax.ppermute(there, "grp", SWAP)]
    step = 1
    while step < tp:
        latent = add([[(array, 0) for array in latents]], order)[0]
        latents = [latent, across(latent, step)]
        step *= 2
    second_other = relay(second_other, order)
    seconds = [
        second,
        second_other,
        lax.ppermute(second, "grp", SWAP),
        lax.ppermute(second_other, "grp", SWAP),
    ]
    return finish(latents, adapter, seconds, terms[0], y, g)


def solution(mesh):
    return jax.shard_map(
        local,
        mesh=mesh,
        in_specs=(
            P(("rep", "grp"), "tp"),
            P(("rep", "grp"), None),
            P("tp", None),
            P(("tp", "grp"), None, None),
            P(("tp", "grp"), None, None),
        ),
        out_specs=P(("rep", "grp"), "tp"),
        check_vma=False,
    )
```

```python
import jax
import jax.numpy as jnp
from jax import lax
from jax.experimental import pallas as pl
from jax.experimental.pallas import tpu as pltpu
from jax.sharding import PartitionSpec as P

SWAP = ((0, 1), (1, 0))
ANY = pl.BlockSpec(memory_space=pl.ANY)
VMEM = pl.BlockSpec(memory_space=pltpu.VMEM)
SMEM = pl.BlockSpec(memory_space=pltpu.SMEM)
TAG_ROWS = 16
COST = pl.CostEstimate(flops=1, bytes_accessed=1, transcendentals=0)
PARAMS = pltpu.CompilerParams(vmem_limit_bytes=64 * 2**20)


class Order:
    def __init__(self, array):
        self.last = array


def block_products(hidden, weight, t, sent, kept, columns, order):
    rows, depth = hidden.shape

    def kernel(t_ref, hidden_ref, weight_ref, after_ref, *out_refs):
        product = jnp.dot(hidden_ref[...], weight_ref[...], preferred_element_type=jnp.float32)
        for i in range(len(sent)):

            @pl.when(pl.program_id(0) == i)
            def _():
                out_refs[i][0] = product.astype(jnp.bfloat16)

        if kept:

            @pl.when(pl.program_id(0) >= len(sent))
            def _():
                out_refs[-1][0] = product

    def block(b, t_ref):
        j = jnp.where(
            b < len(sent),
            (sent[0] if sent else 0) - 2 * b,
            (kept[0] if kept else 0) - 2 * (b - len(sent)),
        )
        return 0, t_ref[0] ^ j

    out_shape = [jax.ShapeDtypeStruct((1, rows, columns), jnp.bfloat16)] * len(sent)
    out_specs = [pl.BlockSpec((1, rows, columns), lambda b, _: (0, 0, 0))] * len(sent)
    if kept:
        out_shape.append(jax.ShapeDtypeStruct((len(kept), rows, columns), jnp.float32))
        out_specs.append(
            pl.BlockSpec((1, rows, columns), lambda b, _: (jnp.maximum(b - len(sent), 0), 0, 0))
        )
    outs = pl.pallas_call(
        kernel,
        name="products",
        out_shape=out_shape,
        grid_spec=pltpu.PrefetchScalarGridSpec(
            num_scalar_prefetch=1,
            grid=(len(sent) + len(kept),),
            in_specs=[
                pl.BlockSpec((rows, depth), lambda b, _: (0, 0)),
                pl.BlockSpec((depth, columns), block),
                ANY,
            ],
            out_specs=out_specs,
        ),
        compiler_params=PARAMS,
        cost_estimate=COST,
    )(t.reshape(1), hidden, weight, order.last)
    order.last = outs[-1]
    return outs


def pack_factors(first, second, tp, y):
    rank = first.shape[0]
    widths = [first.shape[1] // (2 * tp), second.shape[1] // (2 * tp)]
    if widths[0] % 128 or widths[1] % 128:
        parts = [
            lax.dynamic_index_in_dim(
                source.reshape(rank, tp, 2, width), y, 2, keepdims=False
            ).transpose(1, 0, 2)
            for source, width in zip((first, second), widths)
        ]
        return jnp.concatenate(parts, axis=2)
    places = [pl.ds(0, widths[0]), pl.ds(widths[0], widths[1])]

    def kernel(y_ref, first_ref, second_ref, out_ref, buffer, in_sem, out_sem):
        def fetch(i, which):
            width = widths[which]
            start = pl.multiple_of((2 * i + y_ref[0]) * width, 128)
            return pltpu.make_async_copy(
                (first_ref, second_ref)[which].at[:, pl.ds(start, width)],
                buffer.at[i, :, places[which]],
                in_sem.at[i, which],
            )

        def store(i):
            return pltpu.make_async_copy(buffer.at[i], out_ref.at[i], out_sem.at[i])

        for i in range(tp):
            for which in range(2):
                fetch(i, which).start()
        for i in range(tp):
            for which in range(2):
                fetch(i, which).wait()
            store(i).start()
        for i in range(tp):
            store(i).wait()

    shape = (tp, rank, sum(widths))
    return pl.pallas_call(
        kernel,
        name="pack_factors",
        out_shape=jax.ShapeDtypeStruct(shape, first.dtype),
        in_specs=[SMEM, ANY, ANY],
        out_specs=ANY,
        scratch_shapes=[
            pltpu.VMEM(shape, first.dtype),
            pltpu.SemaphoreType.DMA((tp, 2)),
            pltpu.SemaphoreType.DMA((tp,)),
        ],
        compiler_params=PARAMS,
        cost_estimate=COST,
    )(y.reshape(1), first, second)


def pack_hidden(hidden, adapter, half, y, order):
    rows = hidden.shape[0]
    if half % 128 or half < rows:
        tags = jnp.pad(adapter[0], (0, -rows % half)).astype(jnp.bfloat16).reshape(-1, half)
        tags = jnp.pad(tags, ((0, TAG_ROWS - tags.shape[0]), (0, 0)))
        return [
            jnp.concatenate(
                [lax.dynamic_slice(hidden, (0, which * half), (rows, half)), tags], axis=0
            )
            for which in (y, 1 - y)
        ]

    def kernel(y_ref, hidden_ref, adapter_ref, after_ref, mine_ref, other_ref, buffer, in_sem, out_sem):
        def fetch(which):
            half_index = y_ref[0] if which == 0 else 1 - y_ref[0]
            return pltpu.make_async_copy(
                hidden_ref.at[:, pl.ds(pl.multiple_of(half_index * half, 128), half)],
                buffer.at[which, pl.ds(0, rows)],
                in_sem.at[which],
            )

        def store(which):
            out_ref = (mine_ref, other_ref)[which]
            return pltpu.make_async_copy(buffer.at[which], out_ref, out_sem.at[which])

        for which in (1, 0):
            fetch(which).start()
        tags = adapter_ref[...].astype(jnp.float32).astype(hidden.dtype)
        for which in (1, 0):
            buffer[which, rows:, :rows] = jnp.broadcast_to(tags, (TAG_ROWS, rows))
        for which in (1, 0):
            fetch(which).wait()
            store(which).start()
        for which in (1, 0):
            store(which).wait()

    shape = jax.ShapeDtypeStruct((rows + TAG_ROWS, half), hidden.dtype)
    mine, other = pl.pallas_call(
        kernel,
        name="pack_hidden",
        out_shape=[shape, shape],
        in_specs=[SMEM, ANY, VMEM, ANY],
        out_specs=[ANY, ANY],
        scratch_shapes=[
            pltpu.VMEM((2, rows + TAG_ROWS, half), hidden.dtype),
            pltpu.SemaphoreType.DMA((2,)),
            pltpu.SemaphoreType.DMA((2,)),
        ],
        compiler_params=PARAMS,
        cost_estimate=COST,
    )(y.reshape(1), hidden, adapter, order.last)
    order.last = mine
    return mine, other


def latent_terms(factors, half, blocks, rows, rank, g, order):
    count = factors.shape[0]
    tp = count // rank
    pairs = len(blocks) // 2

    def term(factor, rows_held, adapter, core):
        full = lax.dot_general(
            factor, rows_held, (((1,), (1,)), ((), ())), preferred_element_type=jnp.float32
        )
        total = jnp.zeros((rank, rows), jnp.float32)
        for place in range(tp):
            total += jnp.where(
                adapter == place * 2 + core, full[place * rank : (place + 1) * rank], 0.0
            )
        return total

    if half % 128 or half < rows:
        outs = [
            term(
                factors[:, :half],
                block[:rows],
                block[rows:].reshape(-1)[:rows][None].astype(jnp.int32),
                g,
            )
            for block in blocks
        ]
        return jnp.stack(outs[:pairs]), jnp.stack(outs[pairs:]), factors[:, half:]

    def kernel(g_ref, factors_ref, *refs):
        block_refs, out_refs = refs[: len(blocks)], refs[len(blocks) + 1 :]
        for i, block_ref in enumerate(block_refs):
            tag = block_ref[rows:, :rows].astype(jnp.float32)[0:1].astype(jnp.int32)
            out_refs[i // pairs][i % pairs] = term(
                factors_ref[:, :half], block_ref[:rows, :], tag, g_ref[0]
            )
        out_refs[-1][...] = factors_ref[:, half:]

    outs = pl.pallas_call(
        kernel,
        name="latent_terms",
        out_shape=[jax.ShapeDtypeStruct((pairs, rank, rows), jnp.float32)] * 2
        + [jax.ShapeDtypeStruct((count, factors.shape[1] - half), factors.dtype)],
        in_specs=[SMEM, VMEM] + [VMEM] * len(blocks) + [ANY],
        out_specs=[VMEM] * 3,
        compiler_params=PARAMS,
        cost_estimate=COST,
    )(g.reshape(1), factors, *blocks, order.last)
    order.last = outs[0]
    return outs


def block_specs(blocks):
    return [
        pl.BlockSpec((1, *array.shape[1:]), lambda b, i=i: (i, 0, 0)) for array, i in blocks
    ]


def fold(sums, order, pair=()):
    blocks = [block for terms in sums for block in terms]
    shape = blocks[0][0].shape[1:]

    def kernel(*refs):
        at = 0
        outs = refs[len(blocks) + len(pair) + 1 :]
        for out_ref, terms in zip(outs, sums):
            total = refs[at][0]
            for ref in refs[at + 1 : at + len(terms)]:
                total += ref[0].astype(jnp.float32)
            out_ref[0] = total.astype(jnp.bfloat16)
            at += len(terms)
        if pair:
            count = pair[0].shape[0]
            outs[-1][:count] = refs[at][...]
            outs[-1][count:] = refs[at + 1][...]

    out_shape = [jax.ShapeDtypeStruct((1, *shape), jnp.bfloat16)] * len(sums)
    out_specs = [pl.BlockSpec((1, *shape), lambda b: (0, 0, 0))] * len(sums)
    if pair:
        count, width = pair[0].shape
        out_shape.append(jax.ShapeDtypeStruct((2 * count, width), pair[0].dtype))
        out_specs.append(pl.BlockSpec((2 * count, width), lambda b: (0, 0)))
    outs = pl.pallas_call(
        kernel,
        name="fold",
        grid=(1,),
        out_shape=out_shape,
        in_specs=block_specs(blocks)
        + [pl.BlockSpec(array.shape, lambda b: (0, 0)) for array in pair]
        + [ANY],
        out_specs=out_specs,
        compiler_params=PARAMS,
        cost_estimate=COST,
    )(*[array for array, _ in blocks], *pair, order.last)
    order.last = outs[0]
    return outs


def relay(array, after):
    def kernel(array_ref, after_ref, out_ref):
        del array_ref, after_ref, out_ref

    return pl.pallas_call(
        kernel,
        name="relay",
        out_shape=jax.ShapeDtypeStruct(array.shape, array.dtype),
        in_specs=[ANY, ANY],
        out_specs=ANY,
        input_output_aliases={0: 0},
        compiler_params=PARAMS,
        cost_estimate=COST,
    )(array, after)


def finish(latent, adapter, seconds, blocks, y, g):
    rows, columns = blocks[0][0].shape[1:]
    rank = latent.shape[0]
    tp = seconds[0].shape[0] // (2 * rank)
    half = columns // 2

    def spread(held, ids, core):
        held = held.astype(jnp.bfloat16).astype(jnp.float32)
        return jnp.concatenate(
            [
                jnp.where(ids == place * 2 + which, held, jnp.zeros_like(held))
                for which in (core, 1 - core)
                for place in range(tp)
            ],
            axis=0,
        ).astype(jnp.bfloat16)

    def product(left, right):
        return lax.dot_general(
            left, right, (((0,), (0,)), ((), ())), preferred_element_type=jnp.float32
        )

    if half % 128:
        wide = spread(latent, adapter, g)
        mine, other = product(wide, seconds[0]), product(wide, seconds[1])
        delta = jnp.where(
            y == 0,
            jnp.concatenate([mine, other], axis=1),
            jnp.concatenate([other, mine], axis=1),
        )
        total = delta.astype(jnp.bfloat16).astype(jnp.float32)
        for array, i in blocks:
            total = total + array[i].astype(jnp.float32)
        return total.astype(jnp.bfloat16)

    def kernel(y_ref, g_ref, latent_ref, adapter_ref, *refs):
        second_refs, block_refs, out_ref = refs[:2], refs[2:-1], refs[-1]
        wide = spread(latent_ref[...], adapter_ref[...], g_ref[0])
        for which in range(2):
            index = y_ref[0] if which == 0 else 1 - y_ref[0]
            lanes = pl.ds(pl.multiple_of(index * half, 128), half)
            delta = product(wide, second_refs[which][...])
            total = block_refs[0][0, :, lanes]
            for block_ref in block_refs[1:]:
                total += block_ref[0, :, lanes].astype(jnp.float32)
            total += delta.astype(jnp.bfloat16).astype(jnp.float32)
            out_ref[:, lanes] = total.astype(jnp.bfloat16)

    whole = lambda array: pl.BlockSpec(array.shape, lambda b: (0,) * array.ndim)
    return pl.pallas_call(
        kernel,
        name="finish",
        grid=(1,),
        out_shape=jax.ShapeDtypeStruct((rows, columns), jnp.bfloat16),
        in_specs=[SMEM, SMEM]
        + [whole(array) for array in (latent, adapter, *seconds)]
        + block_specs(blocks),
        out_specs=pl.BlockSpec((rows, columns), lambda b: (0, 0)),
        compiler_params=PARAMS,
        cost_estimate=COST,
    )(y.reshape(1), g.reshape(1), latent, adapter, *seconds, *[array for array, _ in blocks])


def local(
    hidden, row_adapter_index, down_projection_weight, adapter_first_factor, adapter_second_factor
):
    tp = lax.axis_size("tp")
    t = lax.axis_index("tp")
    y = lax.axis_index("rep")
    g = lax.axis_index("grp")
    rows, depth = hidden.shape
    rank = adapter_first_factor.shape[2]
    columns = down_projection_weight.shape[1] // tp
    half = depth // 2
    adapter = row_adapter_index.T

    def across(array, step):
        return lax.ppermute(array, "tp", [(i, i ^ step) for i in range(tp)])

    factors = pack_factors(adapter_first_factor[0].T, adapter_second_factor[0], tp, y)
    order = Order(factors)
    factors = lax.all_to_all(factors, "tp", split_axis=0, concat_axis=0, tiled=True)
    factors = factors.reshape(tp * rank, factors.shape[2])
    mine, other = pack_hidden(hidden, adapter, half, y, order)
    from_rep = lax.ppermute(other, "rep", SWAP)
    from_grp = lax.ppermute(mine, "grp", SWAP)
    from_both = lax.ppermute(other, ("rep", "grp"), [(i, 3 - i) for i in range(4)])

    terms = {j: [] for j in range(0, tp, 2)}

    def multiply(sent, kept):
        outs = block_products(hidden, down_projection_weight, t, sent, kept, columns, order)
        for i, j in enumerate(kept):
            terms[j].insert(0, (outs[-1], i))
        for j, out in zip(sent, outs):
            terms[j ^ 1].append((across(out, 1), 0))

    def pass_on(items, pair=()):
        outs = fold([terms[j] for _, j in items], order, pair)
        for (step, j), out in zip(items, outs):
            terms[j ^ step].append((across(out, step), 0))
        return outs[-1]

    odd = list(range(tp - 1, 0, -2))
    stages = []
    step = 2
    while step < tp:
        stages.append([(step, j) for j in range(tp - step, 0, -2 * step)])
        step *= 2

    multiply(odd[:1], [])
    multiply(odd[1:2], [odd[0] - 1])
    multiply(odd[2:3], [odd[1] - 1])
    multiply(odd[3:], [j - 1 for j in odd[2:]])
    pass_on(stages[0][:1])

    blocks = [mine, from_grp, from_rep, from_both]
    near, away, second = latent_terms(factors, half, blocks, rows, rank, g, order)
    got = lax.ppermute(away, "rep", SWAP)
    rest = [stages[0][1:], *stages[1:]]
    if tp <= 8:
        rest = [[item for items in reversed(rest) for item in items]]
    for items in rest[:-1]:
        pass_on(items)
    second = pass_on(rest[-1], (second, lax.ppermute(second, "grp", SWAP)))
    second = relay(second, got)
    seconds = [second, lax.ppermute(second, "rep", SWAP)]

    def exchange(near, got):
        held = near + got
        latent = held[0] + lax.ppermute(held[1], "grp", SWAP)
        step = 1
        while step < tp:
            latent = latent + across(latent, step)
            step *= 2
        return latent

    latent = lax.cond(t < tp, exchange, lambda near, got: near[0], relay(near, order.last), got)
    return finish(latent, adapter, seconds, terms[0], y, g)


def solution(mesh):
    return jax.shard_map(
        local,
        mesh=mesh,
        in_specs=(
            P(("rep", "grp"), "tp"),
            P(("rep", "grp"), None),
            P("tp", None),
            P(("tp", "grp"), None, None),
            P(("tp", "grp"), None, None),
        ),
        out_specs=P(("rep", "grp"), "tp"),
        check_vma=False,
    )
```

```python
import jax
import jax.numpy as jnp
from jax import lax
from jax.experimental import pallas as pl
from jax.experimental.pallas import tpu as pltpu
from jax.sharding import PartitionSpec as P

SWAP = ((0, 1), (1, 0))
ANY = pl.BlockSpec(memory_space=pl.ANY)
VMEM = pl.BlockSpec(memory_space=pltpu.VMEM)
SMEM = pl.BlockSpec(memory_space=pltpu.SMEM)
TAG_ROWS = 16
COST = pl.CostEstimate(flops=1, bytes_accessed=1, transcendentals=0)
PARAMS = pltpu.CompilerParams(vmem_limit_bytes=64 * 2**20)


class Order:
    def __init__(self, array):
        self.last = array


def block_products(hidden, weight, t, sent, kept, columns, order):
    rows, depth = hidden.shape

    def kernel(t_ref, hidden_ref, weight_ref, after_ref, *out_refs):
        product = jnp.dot(hidden_ref[...], weight_ref[...], preferred_element_type=jnp.float32)
        for i in range(len(sent)):

            @pl.when(pl.program_id(0) == i)
            def _():
                out_refs[i][0] = product.astype(jnp.bfloat16)

        if kept:

            @pl.when(pl.program_id(0) >= len(sent))
            def _():
                out_refs[-1][0] = product

    def block(b, t_ref):
        j = jnp.where(
            b < len(sent),
            (sent[0] if sent else 0) - 2 * b,
            (kept[0] if kept else 0) - 2 * (b - len(sent)),
        )
        return 0, t_ref[0] ^ j

    out_shape = [jax.ShapeDtypeStruct((1, rows, columns), jnp.bfloat16)] * len(sent)
    out_specs = [pl.BlockSpec((1, rows, columns), lambda b, _: (0, 0, 0))] * len(sent)
    if kept:
        out_shape.append(jax.ShapeDtypeStruct((len(kept), rows, columns), jnp.float32))
        out_specs.append(
            pl.BlockSpec((1, rows, columns), lambda b, _: (jnp.maximum(b - len(sent), 0), 0, 0))
        )
    outs = pl.pallas_call(
        kernel,
        name="products",
        out_shape=out_shape,
        grid_spec=pltpu.PrefetchScalarGridSpec(
            num_scalar_prefetch=1,
            grid=(len(sent) + len(kept),),
            in_specs=[
                pl.BlockSpec((rows, depth), lambda b, _: (0, 0)),
                pl.BlockSpec((depth, columns), block),
                ANY,
            ],
            out_specs=out_specs,
        ),
        compiler_params=PARAMS,
        cost_estimate=COST,
    )(t.reshape(1), hidden, weight, order.last)
    order.last = outs[-1]
    return outs


def pack_factors(first, second, tp, y):
    rank = first.shape[0]
    widths = [first.shape[1] // (2 * tp), second.shape[1] // (2 * tp)]
    if widths[0] % 128 or widths[1] % 128:
        parts = [
            lax.dynamic_index_in_dim(
                source.reshape(rank, tp, 2, width), y, 2, keepdims=False
            ).transpose(1, 0, 2)
            for source, width in zip((first, second), widths)
        ]
        return jnp.concatenate(parts, axis=2)
    places = [pl.ds(0, widths[0]), pl.ds(widths[0], widths[1])]

    def kernel(y_ref, first_ref, second_ref, out_ref, buffer, in_sem, out_sem):
        def fetch(i, which):
            width = widths[which]
            start = pl.multiple_of((2 * i + y_ref[0]) * width, 128)
            return pltpu.make_async_copy(
                (first_ref, second_ref)[which].at[:, pl.ds(start, width)],
                buffer.at[i, :, places[which]],
                in_sem.at[i, which],
            )

        def store(i):
            return pltpu.make_async_copy(buffer.at[i], out_ref.at[i], out_sem.at[i])

        for i in range(tp):
            for which in range(2):
                fetch(i, which).start()
        for i in range(tp):
            for which in range(2):
                fetch(i, which).wait()
            store(i).start()
        for i in range(tp):
            store(i).wait()

    shape = (tp, rank, sum(widths))
    return pl.pallas_call(
        kernel,
        name="pack_factors",
        out_shape=jax.ShapeDtypeStruct(shape, first.dtype),
        in_specs=[SMEM, ANY, ANY],
        out_specs=ANY,
        scratch_shapes=[
            pltpu.VMEM(shape, first.dtype),
            pltpu.SemaphoreType.DMA((tp, 2)),
            pltpu.SemaphoreType.DMA((tp,)),
        ],
        compiler_params=PARAMS,
        cost_estimate=COST,
    )(y.reshape(1), first, second)


def pack_hidden(hidden, adapter, half, y, order):
    rows = hidden.shape[0]
    if half % 128 or half < rows:
        tags = jnp.pad(adapter[0], (0, -rows % half)).astype(jnp.bfloat16).reshape(-1, half)
        tags = jnp.pad(tags, ((0, TAG_ROWS - tags.shape[0]), (0, 0)))
        return [
            jnp.concatenate(
                [lax.dynamic_slice(hidden, (0, which * half), (rows, half)), tags], axis=0
            )
            for which in (y, 1 - y)
        ]

    def kernel(y_ref, hidden_ref, adapter_ref, after_ref, mine_ref, other_ref, buffer, in_sem, out_sem):
        def fetch(which):
            half_index = y_ref[0] if which == 0 else 1 - y_ref[0]
            return pltpu.make_async_copy(
                hidden_ref.at[:, pl.ds(pl.multiple_of(half_index * half, 128), half)],
                buffer.at[which, pl.ds(0, rows)],
                in_sem.at[which],
            )

        def store(which):
            out_ref = (mine_ref, other_ref)[which]
            return pltpu.make_async_copy(buffer.at[which], out_ref, out_sem.at[which])

        for which in (1, 0):
            fetch(which).start()
        tags = adapter_ref[...].astype(jnp.float32).astype(hidden.dtype)
        for which in (1, 0):
            buffer[which, rows:, :rows] = jnp.broadcast_to(tags, (TAG_ROWS, rows))
        for which in (1, 0):
            fetch(which).wait()
            store(which).start()
        for which in (1, 0):
            store(which).wait()

    shape = jax.ShapeDtypeStruct((rows + TAG_ROWS, half), hidden.dtype)
    mine, other = pl.pallas_call(
        kernel,
        name="pack_hidden",
        out_shape=[shape, shape],
        in_specs=[SMEM, ANY, VMEM, ANY],
        out_specs=[ANY, ANY],
        scratch_shapes=[
            pltpu.VMEM((2, rows + TAG_ROWS, half), hidden.dtype),
            pltpu.SemaphoreType.DMA((2,)),
            pltpu.SemaphoreType.DMA((2,)),
        ],
        compiler_params=PARAMS,
        cost_estimate=COST,
    )(y.reshape(1), hidden, adapter, order.last)
    order.last = mine
    return mine, other


def latent_terms(factors, half, blocks, rows, rank, g, order):
    count = factors.shape[0]
    tp = count // rank
    pairs = len(blocks) // 2

    def term(factor, rows_held, adapter, core):
        full = lax.dot_general(
            factor, rows_held, (((1,), (1,)), ((), ())), preferred_element_type=jnp.float32
        )
        total = jnp.zeros((rank, rows), jnp.float32)
        for place in range(tp):
            total += jnp.where(
                adapter == place * 2 + core, full[place * rank : (place + 1) * rank], 0.0
            )
        return total

    if half % 128 or half < rows:
        outs = [
            term(
                factors[:, :half],
                block[:rows],
                block[rows:].reshape(-1)[:rows][None].astype(jnp.int32),
                g,
            )
            for block in blocks
        ]
        return jnp.stack(outs[:pairs]), jnp.stack(outs[pairs:]), factors[:, half:]

    def kernel(g_ref, factors_ref, *refs):
        block_refs, out_refs = refs[: len(blocks)], refs[len(blocks) + 1 :]
        for i, block_ref in enumerate(block_refs):
            tag = block_ref[rows:, :rows].astype(jnp.float32)[0:1].astype(jnp.int32)
            out_refs[i // pairs][i % pairs] = term(
                factors_ref[:, :half], block_ref[:rows, :], tag, g_ref[0]
            )
        out_refs[-1][...] = factors_ref[:, half:]

    outs = pl.pallas_call(
        kernel,
        name="latent_terms",
        out_shape=[jax.ShapeDtypeStruct((pairs, rank, rows), jnp.float32)] * 2
        + [jax.ShapeDtypeStruct((count, factors.shape[1] - half), factors.dtype)],
        in_specs=[SMEM, VMEM] + [VMEM] * len(blocks) + [ANY],
        out_specs=[VMEM] * 3,
        compiler_params=PARAMS,
        cost_estimate=COST,
    )(g.reshape(1), factors, *blocks, order.last)
    order.last = outs[0]
    return outs


def block_specs(blocks):
    return [
        pl.BlockSpec((1, *array.shape[1:]), lambda b, i=i: (i, 0, 0)) for array, i in blocks
    ]


def fold(sums, order, pair=()):
    blocks = [block for terms in sums for block in terms]
    shape = blocks[0][0].shape[1:]

    def kernel(*refs):
        at = 0
        outs = refs[len(blocks) + len(pair) + 1 :]
        for out_ref, terms in zip(outs, sums):
            total = refs[at][0]
            for ref in refs[at + 1 : at + len(terms)]:
                total += ref[0].astype(jnp.float32)
            out_ref[0] = total.astype(jnp.bfloat16)
            at += len(terms)
        if pair:
            count = pair[0].shape[0]
            outs[-1][:count] = refs[at][...]
            outs[-1][count:] = refs[at + 1][...]

    out_shape = [jax.ShapeDtypeStruct((1, *shape), jnp.bfloat16)] * len(sums)
    out_specs = [pl.BlockSpec((1, *shape), lambda b: (0, 0, 0))] * len(sums)
    if pair:
        count, width = pair[0].shape
        out_shape.append(jax.ShapeDtypeStruct((2 * count, width), pair[0].dtype))
        out_specs.append(pl.BlockSpec((2 * count, width), lambda b: (0, 0)))
    outs = pl.pallas_call(
        kernel,
        name="fold",
        grid=(1,),
        out_shape=out_shape,
        in_specs=block_specs(blocks)
        + [pl.BlockSpec(array.shape, lambda b: (0, 0)) for array in pair]
        + [ANY],
        out_specs=out_specs,
        compiler_params=PARAMS,
        cost_estimate=COST,
    )(*[array for array, _ in blocks], *pair, order.last)
    order.last = outs[0]
    return outs


def relay(array, *after):
    def kernel(*refs):
        del refs

    return pl.pallas_call(
        kernel,
        name="relay",
        out_shape=jax.ShapeDtypeStruct(array.shape, array.dtype),
        in_specs=[ANY] * (1 + len(after)),
        out_specs=ANY,
        input_output_aliases={0: 0},
        compiler_params=PARAMS,
        cost_estimate=COST,
    )(array, *after)


def finish(latent, adapter, seconds, blocks, y, g):
    rows, columns = blocks[0][0].shape[1:]
    rank = latent.shape[0]
    tp = seconds[0].shape[0] // (2 * rank)
    half = columns // 2

    def spread(held, ids, core):
        held = held.astype(jnp.bfloat16).astype(jnp.float32)
        return jnp.concatenate(
            [
                jnp.where(ids == place * 2 + which, held, jnp.zeros_like(held))
                for which in (core, 1 - core)
                for place in range(tp)
            ],
            axis=0,
        ).astype(jnp.bfloat16)

    def product(left, right):
        return lax.dot_general(
            left, right, (((0,), (0,)), ((), ())), preferred_element_type=jnp.float32
        )

    if half % 128:
        wide = spread(latent, adapter, g)
        mine, other = product(wide, seconds[0]), product(wide, seconds[1])
        delta = jnp.where(
            y == 0,
            jnp.concatenate([mine, other], axis=1),
            jnp.concatenate([other, mine], axis=1),
        )
        total = delta.astype(jnp.bfloat16).astype(jnp.float32)
        for array, i in blocks:
            total = total + array[i].astype(jnp.float32)
        return total.astype(jnp.bfloat16)

    def kernel(y_ref, g_ref, latent_ref, adapter_ref, *refs):
        second_refs, block_refs, out_ref = refs[:2], refs[2:-1], refs[-1]
        wide = spread(latent_ref[...], adapter_ref[...], g_ref[0])
        for which in range(2):
            index = y_ref[0] if which == 0 else 1 - y_ref[0]
            lanes = pl.ds(pl.multiple_of(index * half, 128), half)
            delta = product(wide, second_refs[which][...])
            total = block_refs[0][0, :, lanes]
            for block_ref in block_refs[1:]:
                total += block_ref[0, :, lanes].astype(jnp.float32)
            total += delta.astype(jnp.bfloat16).astype(jnp.float32)
            out_ref[:, lanes] = total.astype(jnp.bfloat16)

    whole = lambda array: pl.BlockSpec(array.shape, lambda b: (0,) * array.ndim)
    return pl.pallas_call(
        kernel,
        name="finish",
        grid=(1,),
        out_shape=jax.ShapeDtypeStruct((rows, columns), jnp.bfloat16),
        in_specs=[SMEM, SMEM]
        + [whole(array) for array in (latent, adapter, *seconds)]
        + block_specs(blocks),
        out_specs=pl.BlockSpec((rows, columns), lambda b: (0, 0)),
        compiler_params=PARAMS,
        cost_estimate=COST,
    )(y.reshape(1), g.reshape(1), latent, adapter, *seconds, *[array for array, _ in blocks])


def local(
    hidden, row_adapter_index, down_projection_weight, adapter_first_factor, adapter_second_factor
):
    tp = lax.axis_size("tp")
    t = lax.axis_index("tp")
    y = lax.axis_index("rep")
    g = lax.axis_index("grp")
    rows, depth = hidden.shape
    rank = adapter_first_factor.shape[2]
    columns = down_projection_weight.shape[1] // tp
    half = depth // 2
    adapter = row_adapter_index.T

    def across(array, step):
        return lax.ppermute(array, "tp", [(i, i ^ step) for i in range(tp)])

    factors = pack_factors(adapter_first_factor[0].T, adapter_second_factor[0], tp, y)
    order = Order(factors)
    factors = lax.all_to_all(factors, "tp", split_axis=0, concat_axis=0, tiled=True)
    factors = factors.reshape(tp * rank, factors.shape[2])
    mine, other = pack_hidden(hidden, adapter, half, y, order)
    from_rep = lax.ppermute(other, "rep", SWAP)
    from_grp = lax.ppermute(mine, "grp", SWAP)
    from_both = lax.ppermute(other, ("rep", "grp"), [(i, 3 - i) for i in range(4)])

    terms = {j: [] for j in range(0, tp, 2)}

    def multiply(sent, kept):
        outs = block_products(hidden, down_projection_weight, t, sent, kept, columns, order)
        for i, j in enumerate(kept):
            terms[j].insert(0, (outs[-1], i))
        for j, out in zip(sent, outs):
            terms[j ^ 1].append((across(out, 1), 0))

    def pass_on(items, pair=()):
        outs = fold([terms[j] for _, j in items], order, pair)
        for (step, j), out in zip(items, outs):
            terms[j ^ step].append((across(out, step), 0))
        return outs[-1]

    odd = list(range(tp - 1, 0, -2))
    stages = []
    step = 2
    while step < tp:
        stages.append([(step, j) for j in range(tp - step, 0, -2 * step)])
        step *= 2

    multiply(odd[:1], [])
    multiply(odd[1:2], [odd[0] - 1])
    multiply(odd[2:3], [odd[1] - 1])
    multiply(odd[3:], [j - 1 for j in odd[2:]])
    pass_on(stages[0][:1])

    blocks = [mine, from_grp, from_rep, from_both]
    near, away, second = latent_terms(factors, half, blocks, rows, rank, g, order)
    got = lax.ppermute(away, "rep", SWAP)
    rest = [stages[0][1:], *stages[1:]]
    if tp <= 8:
        rest = [[item for items in reversed(rest) for item in items]]
    for items in rest[:-1]:
        pass_on(items)
    second = pass_on(rest[-1], (second, lax.ppermute(second, "grp", SWAP)))
    second = relay(second, got)
    seconds = [second, lax.ppermute(second, "rep", SWAP)]

    def exchange(near, got):
        held = near + got
        latent = held[0] + lax.ppermute(held[1], "grp", SWAP)
        step = 1
        while step < tp:
            latent = latent + across(latent, step)
            step *= 2
        return latent

    latent = lax.cond(t < tp, exchange, lambda near, got: near[0], relay(near, order.last), got)
    *blocks, (late, i) = terms[0]
    return finish(latent, adapter, seconds, [*blocks, (relay(late, latent), i)], y, g)


def solution(mesh):
    return jax.shard_map(
        local,
        mesh=mesh,
        in_specs=(
            P(("rep", "grp"), "tp"),
            P(("rep", "grp"), None),
            P("tp", None),
            P(("tp", "grp"), None, None),
            P(("tp", "grp"), None, None),
        ),
        out_specs=P(("rep", "grp"), "tp"),
        check_vma=False,
    )
```

```python
import jax
import jax.numpy as jnp
from jax import lax
from jax.experimental import pallas as pl
from jax.experimental.pallas import tpu as pltpu
from jax.sharding import PartitionSpec as P

SWAP = ((0, 1), (1, 0))
ANY = pl.BlockSpec(memory_space=pl.ANY)
VMEM = pl.BlockSpec(memory_space=pltpu.VMEM)
SMEM = pl.BlockSpec(memory_space=pltpu.SMEM)
TAG_ROWS = 16
COST = pl.CostEstimate(flops=1, bytes_accessed=1, transcendentals=0)
PARAMS = pltpu.CompilerParams(vmem_limit_bytes=64 * 2**20)


class Order:
    def __init__(self, array):
        self.last = array


def block_products(hidden, weight, t, sent, kept, columns, order):
    rows, depth = hidden.shape

    def kernel(t_ref, hidden_ref, weight_ref, after_ref, *out_refs):
        product = jnp.dot(hidden_ref[...], weight_ref[...], preferred_element_type=jnp.float32)
        for i in range(len(sent)):

            @pl.when(pl.program_id(0) == i)
            def _():
                out_refs[i][0] = product.astype(jnp.bfloat16)

        if kept:

            @pl.when(pl.program_id(0) >= len(sent))
            def _():
                out_refs[-1][0] = product

    def block(b, t_ref):
        j = jnp.where(
            b < len(sent),
            (sent[0] if sent else 0) - 2 * b,
            (kept[0] if kept else 0) - 2 * (b - len(sent)),
        )
        return 0, t_ref[0] ^ j

    out_shape = [jax.ShapeDtypeStruct((1, rows, columns), jnp.bfloat16)] * len(sent)
    out_specs = [pl.BlockSpec((1, rows, columns), lambda b, _: (0, 0, 0))] * len(sent)
    if kept:
        out_shape.append(jax.ShapeDtypeStruct((len(kept), rows, columns), jnp.float32))
        out_specs.append(
            pl.BlockSpec((1, rows, columns), lambda b, _: (jnp.maximum(b - len(sent), 0), 0, 0))
        )
    outs = pl.pallas_call(
        kernel,
        name="products",
        out_shape=out_shape,
        grid_spec=pltpu.PrefetchScalarGridSpec(
            num_scalar_prefetch=1,
            grid=(len(sent) + len(kept),),
            in_specs=[
                pl.BlockSpec((rows, depth), lambda b, _: (0, 0)),
                pl.BlockSpec((depth, columns), block),
                ANY,
            ],
            out_specs=out_specs,
        ),
        compiler_params=PARAMS,
        cost_estimate=COST,
    )(t.reshape(1), hidden, weight, order.last)
    order.last = outs[-1]
    return outs


def pack_factors(first, second, tp, y):
    rank = first.shape[0]
    widths = [first.shape[1] // (2 * tp), second.shape[1] // (2 * tp)]
    if widths[0] % 128 or widths[1] % 128:
        parts = [
            lax.dynamic_index_in_dim(
                source.reshape(rank, tp, 2, width), y, 2, keepdims=False
            ).transpose(1, 0, 2)
            for source, width in zip((first, second), widths)
        ]
        return jnp.concatenate(parts, axis=2)
    places = [pl.ds(0, widths[0]), pl.ds(widths[0], widths[1])]

    def kernel(y_ref, first_ref, second_ref, out_ref, buffer, in_sem, out_sem):
        def fetch(i, which):
            width = widths[which]
            start = pl.multiple_of((2 * i + y_ref[0]) * width, 128)
            return pltpu.make_async_copy(
                (first_ref, second_ref)[which].at[:, pl.ds(start, width)],
                buffer.at[i, :, places[which]],
                in_sem.at[i, which],
            )

        def store(i):
            return pltpu.make_async_copy(buffer.at[i], out_ref.at[i], out_sem.at[i])

        for i in range(tp):
            for which in range(2):
                fetch(i, which).start()
        for i in range(tp):
            for which in range(2):
                fetch(i, which).wait()
            store(i).start()
        for i in range(tp):
            store(i).wait()

    shape = (tp, rank, sum(widths))
    return pl.pallas_call(
        kernel,
        name="pack_factors",
        out_shape=jax.ShapeDtypeStruct(shape, first.dtype),
        in_specs=[SMEM, ANY, ANY],
        out_specs=ANY,
        scratch_shapes=[
            pltpu.VMEM(shape, first.dtype),
            pltpu.SemaphoreType.DMA((tp, 2)),
            pltpu.SemaphoreType.DMA((tp,)),
        ],
        compiler_params=PARAMS,
        cost_estimate=COST,
    )(y.reshape(1), first, second)


def pack_hidden(hidden, adapter, half, y, order):
    rows = hidden.shape[0]
    if half % 128 or half < rows:
        tags = jnp.pad(adapter[0], (0, -rows % half)).astype(jnp.bfloat16).reshape(-1, half)
        tags = jnp.pad(tags, ((0, TAG_ROWS - tags.shape[0]), (0, 0)))
        return [
            jnp.concatenate(
                [lax.dynamic_slice(hidden, (0, which * half), (rows, half)), tags], axis=0
            )
            for which in (y, 1 - y)
        ]

    def kernel(y_ref, hidden_ref, adapter_ref, after_ref, mine_ref, other_ref, buffer, in_sem, out_sem):
        def fetch(which):
            half_index = y_ref[0] if which == 0 else 1 - y_ref[0]
            return pltpu.make_async_copy(
                hidden_ref.at[:, pl.ds(pl.multiple_of(half_index * half, 128), half)],
                buffer.at[which, pl.ds(0, rows)],
                in_sem.at[which],
            )

        def store(which):
            out_ref = (mine_ref, other_ref)[which]
            return pltpu.make_async_copy(buffer.at[which], out_ref, out_sem.at[which])

        for which in (1, 0):
            fetch(which).start()
        tags = adapter_ref[...].astype(jnp.float32).astype(hidden.dtype)
        for which in (1, 0):
            buffer[which, rows:, :rows] = jnp.broadcast_to(tags, (TAG_ROWS, rows))
        for which in (1, 0):
            fetch(which).wait()
            store(which).start()
        for which in (1, 0):
            store(which).wait()

    shape = jax.ShapeDtypeStruct((rows + TAG_ROWS, half), hidden.dtype)
    mine, other = pl.pallas_call(
        kernel,
        name="pack_hidden",
        out_shape=[shape, shape],
        in_specs=[SMEM, ANY, VMEM, ANY],
        out_specs=[ANY, ANY],
        scratch_shapes=[
            pltpu.VMEM((2, rows + TAG_ROWS, half), hidden.dtype),
            pltpu.SemaphoreType.DMA((2,)),
            pltpu.SemaphoreType.DMA((2,)),
        ],
        compiler_params=PARAMS,
        cost_estimate=COST,
    )(y.reshape(1), hidden, adapter, order.last)
    order.last = mine
    return mine, other


def latent_terms(factors, half, blocks, rows, rank, g, order):
    count = factors.shape[0]
    tp = count // rank
    pairs = len(blocks) // 2

    def term(factor, rows_held, adapter, core):
        full = lax.dot_general(
            factor, rows_held, (((1,), (1,)), ((), ())), preferred_element_type=jnp.float32
        )
        total = jnp.zeros((rank, rows), jnp.float32)
        for place in range(tp):
            total += jnp.where(
                adapter == place * 2 + core, full[place * rank : (place + 1) * rank], 0.0
            )
        return total

    if half % 128 or half < rows:
        outs = [
            term(
                factors[:, :half],
                block[:rows],
                block[rows:].reshape(-1)[:rows][None].astype(jnp.int32),
                g,
            )
            for block in blocks
        ]
        return jnp.stack(outs[:pairs]), jnp.stack(outs[pairs:]), factors[:, half:]

    def kernel(g_ref, factors_ref, *refs):
        block_refs, out_refs = refs[: len(blocks)], refs[len(blocks) + 1 :]
        for i, block_ref in enumerate(block_refs):
            tag = block_ref[rows:, :rows].astype(jnp.float32)[0:1].astype(jnp.int32)
            out_refs[i // pairs][i % pairs] = term(
                factors_ref[:, :half], block_ref[:rows, :], tag, g_ref[0]
            )
        out_refs[-1][...] = factors_ref[:, half:]

    outs = pl.pallas_call(
        kernel,
        name="latent_terms",
        out_shape=[jax.ShapeDtypeStruct((pairs, rank, rows), jnp.float32)] * 2
        + [jax.ShapeDtypeStruct((count, factors.shape[1] - half), factors.dtype)],
        in_specs=[SMEM, VMEM] + [VMEM] * len(blocks) + [ANY],
        out_specs=[VMEM] * 3,
        compiler_params=PARAMS,
        cost_estimate=COST,
    )(g.reshape(1), factors, *blocks, order.last)
    order.last = outs[0]
    return outs


def block_specs(blocks):
    return [
        pl.BlockSpec((1, *array.shape[1:]), lambda b, i=i: (i, 0, 0)) for array, i in blocks
    ]


def fold(sums, order, pair=()):
    blocks = [block for terms in sums for block in terms]
    shape = blocks[0][0].shape[1:]

    def kernel(*refs):
        at = 0
        outs = refs[len(blocks) + len(pair) + 1 :]
        for out_ref, terms in zip(outs, sums):
            total = refs[at][0]
            for ref in refs[at + 1 : at + len(terms)]:
                total += ref[0].astype(jnp.float32)
            out_ref[0] = total.astype(jnp.bfloat16)
            at += len(terms)
        if pair:
            count = pair[0].shape[0]
            outs[-1][:count] = refs[at][...]
            outs[-1][count:] = refs[at + 1][...]

    out_shape = [jax.ShapeDtypeStruct((1, *shape), jnp.bfloat16)] * len(sums)
    out_specs = [pl.BlockSpec((1, *shape), lambda b: (0, 0, 0))] * len(sums)
    if pair:
        count, width = pair[0].shape
        out_shape.append(jax.ShapeDtypeStruct((2 * count, width), pair[0].dtype))
        out_specs.append(pl.BlockSpec((2 * count, width), lambda b: (0, 0)))
    outs = pl.pallas_call(
        kernel,
        name="fold",
        grid=(1,),
        out_shape=out_shape,
        in_specs=block_specs(blocks)
        + [pl.BlockSpec(array.shape, lambda b: (0, 0)) for array in pair]
        + [ANY],
        out_specs=out_specs,
        compiler_params=PARAMS,
        cost_estimate=COST,
    )(*[array for array, _ in blocks], *pair, order.last)
    order.last = outs[0]
    return outs


def relay(array, *after):
    def kernel(*refs):
        del refs

    return pl.pallas_call(
        kernel,
        name="relay",
        out_shape=jax.ShapeDtypeStruct(array.shape, array.dtype),
        in_specs=[ANY] * (1 + len(after)),
        out_specs=ANY,
        input_output_aliases={0: 0},
        compiler_params=PARAMS,
        cost_estimate=COST,
    )(array, *after)


def finish(latent, adapter, seconds, blocks, y, g):
    rows, columns = blocks[0][0].shape[1:]
    rank = latent.shape[0]
    tp = seconds[0].shape[0] // rank
    half = columns // 2

    def spread(held, ids, core):
        held = held.astype(jnp.bfloat16).astype(jnp.float32)
        return jnp.concatenate(
            [jnp.where(ids == place * 2 + core, held, jnp.zeros_like(held)) for place in range(tp)],
            axis=0,
        ).astype(jnp.bfloat16)

    def product(left, right):
        return lax.dot_general(
            left, right, (((0,), (0,)), ((), ())), preferred_element_type=jnp.float32
        )

    if half % 128:
        near, far = spread(latent, adapter, g), spread(latent, adapter, 1 - g)
        mine = product(near, seconds[0]) + product(far, seconds[1])
        other = product(near, seconds[2]) + product(far, seconds[3])
        delta = jnp.where(
            y == 0,
            jnp.concatenate([mine, other], axis=1),
            jnp.concatenate([other, mine], axis=1),
        )
        total = delta.astype(jnp.bfloat16).astype(jnp.float32)
        for array, i in blocks:
            total = total + array[i].astype(jnp.float32)
        return total.astype(jnp.bfloat16)

    def kernel(y_ref, g_ref, latent_ref, adapter_ref, *refs):
        second_refs, block_refs, out_ref = refs[:4], refs[4:-1], refs[-1]
        near = spread(latent_ref[...], adapter_ref[...], g_ref[0])
        far = spread(latent_ref[...], adapter_ref[...], 1 - g_ref[0])
        for which in range(2):
            index = y_ref[0] if which == 0 else 1 - y_ref[0]
            lanes = pl.ds(pl.multiple_of(index * half, 128), half)
            delta = product(near, second_refs[2 * which][...])
            delta += product(far, second_refs[2 * which + 1][...])
            total = block_refs[0][0, :, lanes]
            for block_ref in block_refs[1:]:
                total += block_ref[0, :, lanes].astype(jnp.float32)
            total += delta.astype(jnp.bfloat16).astype(jnp.float32)
            out_ref[:, lanes] = total.astype(jnp.bfloat16)

    whole = lambda array: pl.BlockSpec(array.shape, lambda b: (0,) * array.ndim)
    return pl.pallas_call(
        kernel,
        name="finish",
        grid=(1,),
        out_shape=jax.ShapeDtypeStruct((rows, columns), jnp.bfloat16),
        in_specs=[SMEM, SMEM]
        + [whole(array) for array in (latent, adapter, *seconds)]
        + block_specs(blocks),
        out_specs=pl.BlockSpec((rows, columns), lambda b: (0, 0)),
        compiler_params=PARAMS,
        cost_estimate=COST,
    )(y.reshape(1), g.reshape(1), latent, adapter, *seconds, *[array for array, _ in blocks])


def local(
    hidden, row_adapter_index, down_projection_weight, adapter_first_factor, adapter_second_factor
):
    tp = lax.axis_size("tp")
    t = lax.axis_index("tp")
    y = lax.axis_index("rep")
    g = lax.axis_index("grp")
    rows, depth = hidden.shape
    rank = adapter_first_factor.shape[2]
    columns = down_projection_weight.shape[1] // tp
    half = depth // 2
    adapter = row_adapter_index.T

    def across(array, step):
        return lax.ppermute(array, "tp", [(i, i ^ step) for i in range(tp)])

    factors = pack_factors(adapter_first_factor[0].T, adapter_second_factor[0], tp, y)
    order = Order(factors)
    factors = lax.all_to_all(factors, "tp", split_axis=0, concat_axis=0, tiled=True)
    factors = factors.reshape(tp * rank, factors.shape[2])
    mine, other = pack_hidden(hidden, adapter, half, y, order)
    from_rep = lax.ppermute(other, "rep", SWAP)
    from_grp = lax.ppermute(mine, "grp", SWAP)
    from_both = lax.ppermute(other, ("rep", "grp"), [(i, 3 - i) for i in range(4)])

    terms = {j: [] for j in range(0, tp, 2)}

    def multiply(sent, kept):
        outs = block_products(hidden, down_projection_weight, t, sent, kept, columns, order)
        for i, j in enumerate(kept):
            terms[j].insert(0, (outs[-1], i))
        for j, out in zip(sent, outs):
            terms[j ^ 1].append((across(out, 1), 0))

    def pass_on(items, pair=()):
        outs = fold([terms[j] for _, j in items], order, pair)
        for (step, j), out in zip(items, outs):
            terms[j ^ step].append((across(out, step), 0))
        return outs[-1]

    odd = list(range(tp - 1, 0, -2))
    stages = []
    step = 2
    while step < tp:
        stages.append([(step, j) for j in range(tp - step, 0, -2 * step)])
        step *= 2

    multiply(odd[:1], [])
    multiply(odd[1:2], [odd[0] - 1])
    multiply(odd[2:3], [odd[1] - 1])
    multiply(odd[3:], [j - 1 for j in odd[2:]])
    pass_on(stages[0][:1])

    blocks = [mine, from_grp, from_rep, from_both]
    near, away, second = latent_terms(factors, half, blocks, rows, rank, g, order)
    got = lax.ppermute(away, "rep", SWAP)
    rest = [stages[0][1:], *stages[1:]]
    if tp <= 8:
        rest = [[item] for items in reversed(rest) for item in items]
    for items in rest:
        pass_on(items)

    def inner(near, got):
        held = near + got
        latent = held[0] + lax.ppermute(held[1], "grp", SWAP)
        step = 1
        while 4 * step < tp:
            latent = latent + across(latent, step)
            step *= 2
        return latent

    def outer(latent):
        step = tp // 4
        sent = latent.astype(jnp.bfloat16)
        for i in range(1, 4):
            latent = latent + across(sent, i * step).astype(jnp.float32)
        return latent

    def swap(*arrays):
        return [lax.ppermute(array, "grp", SWAP) for array in arrays]

    latent = lax.cond(t < tp, inner, lambda near, got: near[0], relay(near, order.last), got)
    kept, (r, i), (late, k), *others = terms[0]
    r = relay(r, latent)
    second = relay(second, got)
    second_other = relay(lax.ppermute(second, "rep", SWAP), r)
    twins = lax.cond(t < tp, swap, lambda *arrays: list(arrays), second, second_other)
    latent = lax.cond(t < tp, outer, lambda latent: latent, relay(latent, twins[1]))
    seconds = [second, twins[0], second_other, twins[1]]
    blocks = [kept, (r, i), (relay(late, latent), k), *others]
    return finish(latent, adapter, seconds, blocks, y, g)


def solution(mesh):
    return jax.shard_map(
        local,
        mesh=mesh,
        in_specs=(
            P(("rep", "grp"), "tp"),
            P(("rep", "grp"), None),
            P("tp", None),
            P(("tp", "grp"), None, None),
            P(("tp", "grp"), None, None),
        ),
        out_specs=P(("rep", "grp"), "tp"),
        check_vma=False,
    )
```

```python
import jax
import jax.numpy as jnp
from jax import lax
from jax.experimental import pallas as pl
from jax.experimental.pallas import tpu as pltpu
from jax.sharding import PartitionSpec as P

SWAP = ((0, 1), (1, 0))
ANY = pl.BlockSpec(memory_space=pl.ANY)
VMEM = pl.BlockSpec(memory_space=pltpu.VMEM)
SMEM = pl.BlockSpec(memory_space=pltpu.SMEM)
TAG_ROWS = 16
COST = pl.CostEstimate(flops=1, bytes_accessed=1, transcendentals=0)
PARAMS = pltpu.CompilerParams(vmem_limit_bytes=64 * 2**20)


class Order:
    def __init__(self, array):
        self.last = array


def block_products(hidden, weight, t, sent, kept, columns, order):
    rows, depth = hidden.shape

    def kernel(t_ref, hidden_ref, weight_ref, after_ref, *out_refs):
        product = jnp.dot(hidden_ref[...], weight_ref[...], preferred_element_type=jnp.float32)
        for i in range(len(sent)):

            @pl.when(pl.program_id(0) == i)
            def _():
                out_refs[i][0] = product.astype(jnp.bfloat16)

        if kept:

            @pl.when(pl.program_id(0) >= len(sent))
            def _():
                out_refs[-1][0] = product

    def block(b, t_ref):
        j = jnp.where(
            b < len(sent),
            (sent[0] if sent else 0) - 2 * b,
            (kept[0] if kept else 0) - 2 * (b - len(sent)),
        )
        return 0, t_ref[0] ^ j

    out_shape = [jax.ShapeDtypeStruct((1, rows, columns), jnp.bfloat16)] * len(sent)
    out_specs = [pl.BlockSpec((1, rows, columns), lambda b, _: (0, 0, 0))] * len(sent)
    if kept:
        out_shape.append(jax.ShapeDtypeStruct((len(kept), rows, columns), jnp.float32))
        out_specs.append(
            pl.BlockSpec((1, rows, columns), lambda b, _: (jnp.maximum(b - len(sent), 0), 0, 0))
        )
    outs = pl.pallas_call(
        kernel,
        name="products",
        out_shape=out_shape,
        grid_spec=pltpu.PrefetchScalarGridSpec(
            num_scalar_prefetch=1,
            grid=(len(sent) + len(kept),),
            in_specs=[
                pl.BlockSpec((rows, depth), lambda b, _: (0, 0)),
                pl.BlockSpec((depth, columns), block),
                ANY,
            ],
            out_specs=out_specs,
        ),
        compiler_params=PARAMS,
        cost_estimate=COST,
    )(t.reshape(1), hidden, weight, order.last)
    order.last = outs[-1]
    return outs


def pack_factors(first, second, tp, y):
    rank = first.shape[0]
    widths = [first.shape[1] // (2 * tp), second.shape[1] // (2 * tp)]
    if widths[0] % 128 or widths[1] % 128:
        parts = [
            lax.dynamic_index_in_dim(
                source.reshape(rank, tp, 2, width), y, 2, keepdims=False
            ).transpose(1, 0, 2)
            for source, width in zip((first, second), widths)
        ]
        return jnp.concatenate(parts, axis=2)
    places = [pl.ds(0, widths[0]), pl.ds(widths[0], widths[1])]

    def kernel(y_ref, first_ref, second_ref, out_ref, buffer, in_sem, out_sem):
        def fetch(i, which):
            width = widths[which]
            start = pl.multiple_of((2 * i + y_ref[0]) * width, 128)
            return pltpu.make_async_copy(
                (first_ref, second_ref)[which].at[:, pl.ds(start, width)],
                buffer.at[i, :, places[which]],
                in_sem.at[i, which],
            )

        def store(i):
            return pltpu.make_async_copy(buffer.at[i], out_ref.at[i], out_sem.at[i])

        for i in range(tp):
            for which in range(2):
                fetch(i, which).start()
        for i in range(tp):
            for which in range(2):
                fetch(i, which).wait()
            store(i).start()
        for i in range(tp):
            store(i).wait()

    shape = (tp, rank, sum(widths))
    return pl.pallas_call(
        kernel,
        name="pack_factors",
        out_shape=jax.ShapeDtypeStruct(shape, first.dtype),
        in_specs=[SMEM, ANY, ANY],
        out_specs=ANY,
        scratch_shapes=[
            pltpu.VMEM(shape, first.dtype),
            pltpu.SemaphoreType.DMA((tp, 2)),
            pltpu.SemaphoreType.DMA((tp,)),
        ],
        compiler_params=PARAMS,
        cost_estimate=COST,
    )(y.reshape(1), first, second)


def pack_hidden(hidden, adapter, half, y, order):
    rows = hidden.shape[0]
    if half % 128 or half < rows:
        tags = jnp.pad(adapter[0], (0, -rows % half)).astype(jnp.bfloat16).reshape(-1, half)
        tags = jnp.pad(tags, ((0, TAG_ROWS - tags.shape[0]), (0, 0)))
        return [
            jnp.concatenate(
                [lax.dynamic_slice(hidden, (0, which * half), (rows, half)), tags], axis=0
            )
            for which in (y, 1 - y)
        ]

    def kernel(y_ref, hidden_ref, adapter_ref, after_ref, mine_ref, other_ref, buffer, in_sem, out_sem):
        def fetch(which):
            half_index = y_ref[0] if which == 0 else 1 - y_ref[0]
            return pltpu.make_async_copy(
                hidden_ref.at[:, pl.ds(pl.multiple_of(half_index * half, 128), half)],
                buffer.at[which, pl.ds(0, rows)],
                in_sem.at[which],
            )

        def store(which):
            out_ref = (mine_ref, other_ref)[which]
            return pltpu.make_async_copy(buffer.at[which], out_ref, out_sem.at[which])

        for which in (1, 0):
            fetch(which).start()
        tags = adapter_ref[...].astype(jnp.float32).astype(hidden.dtype)
        for which in (1, 0):
            buffer[which, rows:, :rows] = jnp.broadcast_to(tags, (TAG_ROWS, rows))
        for which in (1, 0):
            fetch(which).wait()
            store(which).start()
        for which in (1, 0):
            store(which).wait()

    shape = jax.ShapeDtypeStruct((rows + TAG_ROWS, half), hidden.dtype)
    mine, other = pl.pallas_call(
        kernel,
        name="pack_hidden",
        out_shape=[shape, shape],
        in_specs=[SMEM, ANY, VMEM, ANY],
        out_specs=[ANY, ANY],
        scratch_shapes=[
            pltpu.VMEM((2, rows + TAG_ROWS, half), hidden.dtype),
            pltpu.SemaphoreType.DMA((2,)),
            pltpu.SemaphoreType.DMA((2,)),
        ],
        compiler_params=PARAMS,
        cost_estimate=COST,
    )(y.reshape(1), hidden, adapter, order.last)
    order.last = mine
    return mine, other


def latent_terms(factors, half, blocks, rows, rank, g, order):
    count = factors.shape[0]
    tp = count // rank
    pairs = len(blocks) // 2

    def term(factor, rows_held, adapter, core):
        full = lax.dot_general(
            factor, rows_held, (((1,), (1,)), ((), ())), preferred_element_type=jnp.float32
        )
        total = jnp.zeros((rank, rows), jnp.float32)
        for place in range(tp):
            total += jnp.where(
                adapter == place * 2 + core, full[place * rank : (place + 1) * rank], 0.0
            )
        return total

    if half % 128 or half < rows:
        outs = [
            term(
                factors[:, :half],
                block[:rows],
                block[rows:].reshape(-1)[:rows][None].astype(jnp.int32),
                g,
            )
            for block in blocks
        ]
        return jnp.stack(outs[:pairs]), jnp.stack(outs[pairs:]), factors[:, half:]

    def kernel(g_ref, factors_ref, *refs):
        block_refs, out_refs = refs[: len(blocks)], refs[len(blocks) + 1 :]
        for i, block_ref in enumerate(block_refs):
            tag = block_ref[rows:, :rows].astype(jnp.float32)[0:1].astype(jnp.int32)
            out_refs[i // pairs][i % pairs] = term(
                factors_ref[:, :half], block_ref[:rows, :], tag, g_ref[0]
            )
        out_refs[-1][...] = factors_ref[:, half:]

    outs = pl.pallas_call(
        kernel,
        name="latent_terms",
        out_shape=[jax.ShapeDtypeStruct((pairs, rank, rows), jnp.float32)] * 2
        + [jax.ShapeDtypeStruct((count, factors.shape[1] - half), factors.dtype)],
        in_specs=[SMEM, VMEM] + [VMEM] * len(blocks) + [ANY],
        out_specs=[VMEM] * 3,
        compiler_params=PARAMS,
        cost_estimate=COST,
    )(g.reshape(1), factors, *blocks, order.last)
    order.last = outs[0]
    return outs


def block_specs(blocks):
    return [
        pl.BlockSpec((1, *array.shape[1:]), lambda b, i=i: (i, 0, 0)) for array, i in blocks
    ]


def fold(sums, order, pair=()):
    blocks = [block for terms in sums for block in terms]
    shape = blocks[0][0].shape[1:]

    def kernel(*refs):
        at = 0
        outs = refs[len(blocks) + len(pair) + 1 :]
        for out_ref, terms in zip(outs, sums):
            total = refs[at][0]
            for ref in refs[at + 1 : at + len(terms)]:
                total += ref[0].astype(jnp.float32)
            out_ref[0] = total.astype(jnp.bfloat16)
            at += len(terms)
        if pair:
            count = pair[0].shape[0]
            outs[-1][:count] = refs[at][...]
            outs[-1][count:] = refs[at + 1][...]

    out_shape = [jax.ShapeDtypeStruct((1, *shape), jnp.bfloat16)] * len(sums)
    out_specs = [pl.BlockSpec((1, *shape), lambda b: (0, 0, 0))] * len(sums)
    if pair:
        count, width = pair[0].shape
        out_shape.append(jax.ShapeDtypeStruct((2 * count, width), pair[0].dtype))
        out_specs.append(pl.BlockSpec((2 * count, width), lambda b: (0, 0)))
    outs = pl.pallas_call(
        kernel,
        name="fold",
        grid=(1,),
        out_shape=out_shape,
        in_specs=block_specs(blocks)
        + [pl.BlockSpec(array.shape, lambda b: (0, 0)) for array in pair]
        + [ANY],
        out_specs=out_specs,
        compiler_params=PARAMS,
        cost_estimate=COST,
    )(*[array for array, _ in blocks], *pair, order.last)
    order.last = outs[0]
    return outs


def relay(array, *after):
    def kernel(*refs):
        del refs

    return pl.pallas_call(
        kernel,
        name="relay",
        out_shape=jax.ShapeDtypeStruct(array.shape, array.dtype),
        in_specs=[ANY] * (1 + len(after)),
        out_specs=ANY,
        input_output_aliases={0: 0},
        compiler_params=PARAMS,
        cost_estimate=COST,
    )(array, *after)


def finish(latents, adapter, seconds, blocks, y, g):
    rows, columns = blocks[0][0].shape[1:]
    rank = latents[0].shape[0]
    tp = seconds[0].shape[0] // rank
    half = columns // 2

    def spread(held, ids, core):
        held = held.astype(jnp.bfloat16).astype(jnp.float32)
        return jnp.concatenate(
            [jnp.where(ids == place * 2 + core, held, jnp.zeros_like(held)) for place in range(tp)],
            axis=0,
        ).astype(jnp.bfloat16)

    def product(left, right):
        return lax.dot_general(
            left, right, (((0,), (0,)), ((), ())), preferred_element_type=jnp.float32
        )

    def total_of(parts):
        total = parts[0]
        for part in parts[1:]:
            total = total + part.astype(jnp.float32)
        return total

    if half % 128:
        latent = total_of(latents)
        near, far = spread(latent, adapter, g), spread(latent, adapter, 1 - g)
        mine = product(near, seconds[0]) + product(far, seconds[1])
        other = product(near, seconds[2]) + product(far, seconds[3])
        delta = jnp.where(
            y == 0,
            jnp.concatenate([mine, other], axis=1),
            jnp.concatenate([other, mine], axis=1),
        )
        total = delta.astype(jnp.bfloat16).astype(jnp.float32)
        for array, i in blocks:
            total = total + array[i].astype(jnp.float32)
        return total.astype(jnp.bfloat16)

    def kernel(y_ref, g_ref, *refs):
        latent_refs, adapter_ref, refs = refs[: len(latents)], refs[len(latents)], refs[len(latents) + 1 :]
        latent = total_of([latent_ref[...] for latent_ref in latent_refs])
        second_refs, block_refs, out_ref = refs[:4], refs[4:-1], refs[-1]
        near = spread(latent, adapter_ref[...], g_ref[0])
        far = spread(latent, adapter_ref[...], 1 - g_ref[0])
        for which in range(2):
            index = y_ref[0] if which == 0 else 1 - y_ref[0]
            lanes = pl.ds(pl.multiple_of(index * half, 128), half)
            delta = product(near, second_refs[2 * which][...])
            delta += product(far, second_refs[2 * which + 1][...])
            total = block_refs[0][0, :, lanes]
            for block_ref in block_refs[1:]:
                total += block_ref[0, :, lanes].astype(jnp.float32)
            total += delta.astype(jnp.bfloat16).astype(jnp.float32)
            out_ref[:, lanes] = total.astype(jnp.bfloat16)

    whole = lambda array: pl.BlockSpec(array.shape, lambda b: (0,) * array.ndim)
    return pl.pallas_call(
        kernel,
        name="finish",
        grid=(1,),
        out_shape=jax.ShapeDtypeStruct((rows, columns), jnp.bfloat16),
        in_specs=[SMEM, SMEM]
        + [whole(array) for array in (*latents, adapter, *seconds)]
        + block_specs(blocks),
        out_specs=pl.BlockSpec((rows, columns), lambda b: (0, 0)),
        compiler_params=PARAMS,
        cost_estimate=COST,
    )(y.reshape(1), g.reshape(1), *latents, adapter, *seconds, *[array for array, _ in blocks])


def local(
    hidden, row_adapter_index, down_projection_weight, adapter_first_factor, adapter_second_factor
):
    tp = lax.axis_size("tp")
    t = lax.axis_index("tp")
    y = lax.axis_index("rep")
    g = lax.axis_index("grp")
    rows, depth = hidden.shape
    rank = adapter_first_factor.shape[2]
    columns = down_projection_weight.shape[1] // tp
    half = depth // 2
    adapter = row_adapter_index.T

    def across(array, step):
        return lax.ppermute(array, "tp", [(i, i ^ step) for i in range(tp)])

    factors = pack_factors(adapter_first_factor[0].T, adapter_second_factor[0], tp, y)
    order = Order(factors)
    factors = lax.all_to_all(factors, "tp", split_axis=0, concat_axis=0, tiled=True)
    factors = factors.reshape(tp * rank, factors.shape[2])
    mine, other = pack_hidden(hidden, adapter, half, y, order)
    from_rep = lax.ppermute(other, "rep", SWAP)
    from_grp = lax.ppermute(mine, "grp", SWAP)
    from_both = lax.ppermute(other, ("rep", "grp"), [(i, 3 - i) for i in range(4)])

    terms = {j: [] for j in range(0, tp, 2)}

    def multiply(sent, kept):
        outs = block_products(hidden, down_projection_weight, t, sent, kept, columns, order)
        for i, j in enumerate(kept):
            terms[j].insert(0, (outs[-1], i))
        for j, out in zip(sent, outs):
            terms[j ^ 1].append((across(out, 1), 0))

    def pass_on(items, pair=()):
        outs = fold([terms[j] for _, j in items], order, pair)
        for (step, j), out in zip(items, outs):
            terms[j ^ step].append((across(out, step), 0))
        return outs[-1]

    odd = list(range(tp - 1, 0, -2))
    stages = []
    step = 2
    while step < tp:
        stages.append([(step, j) for j in range(tp - step, 0, -2 * step)])
        step *= 2

    multiply(odd[:1], [])
    multiply(odd[1:2], [odd[0] - 1])
    multiply(odd[2:], [j - 1 for j in odd[1:]])
    pass_on(stages[0][:1])

    blocks = [mine, from_grp, from_rep, from_both]
    near, away, second = latent_terms(factors, half, blocks, rows, rank, g, order)
    got = lax.ppermute(away, "rep", SWAP)
    rest = [stages[0][1:], *stages[1:]]
    if tp <= 8:
        rest = [[item] for items in reversed(rest) for item in items]
    for items in rest:
        pass_on(items)

    def inner(near, got):
        held = near + got
        latent = held[0] + lax.ppermute(held[1], "grp", SWAP)
        step = 1
        while 4 * step < tp:
            latent = latent + across(latent, step)
            step *= 2
        return latent

    def outer(latent):
        step = tp // 4
        sent = latent.astype(jnp.bfloat16)
        return [across(sent, i * step) for i in range(1, 4)]

    def swap(*arrays):
        return [lax.ppermute(array, "grp", SWAP) for array in arrays]

    latent = lax.cond(t < tp, inner, lambda near, got: near[0], relay(near, order.last), got)
    kept, (r, i), (late, k), *others = terms[0]
    r = relay(r, latent)
    second = relay(second, got)
    second_other = relay(lax.ppermute(second, "rep", SWAP), r)
    twins = lax.cond(t < tp, swap, lambda *arrays: list(arrays), second, second_other)
    latent = relay(latent, twins[1])
    got = lax.cond(t < tp, outer, lambda latent: [latent.astype(jnp.bfloat16)] * 3, latent)
    latents = [latent, *got]
    seconds = [second, twins[0], second_other, twins[1]]
    blocks = [kept, (r, i), (relay(late, got[2]), k), *others]
    return finish(latents, adapter, seconds, blocks, y, g)


def solution(mesh):
    return jax.shard_map(
        local,
        mesh=mesh,
        in_specs=(
            P(("rep", "grp"), "tp"),
            P(("rep", "grp"), None),
            P("tp", None),
            P(("tp", "grp"), None, None),
            P(("tp", "grp"), None, None),
        ),
        out_specs=P(("rep", "grp"), "tp"),
        check_vma=False,
    )
```

```python
import jax
import jax.numpy as jnp
from jax import lax
from jax.experimental import pallas as pl
from jax.experimental.pallas import tpu as pltpu
from jax.sharding import PartitionSpec as P

SWAP = ((0, 1), (1, 0))
ANY = pl.BlockSpec(memory_space=pl.ANY)
VMEM = pl.BlockSpec(memory_space=pltpu.VMEM)
SMEM = pl.BlockSpec(memory_space=pltpu.SMEM)
TAG_ROWS = 16
COST = pl.CostEstimate(flops=1, bytes_accessed=1, transcendentals=0)
PARAMS = pltpu.CompilerParams(vmem_limit_bytes=64 * 2**20)


class Order:
    def __init__(self, array):
        self.last = array


def block_products(hidden, weight, t, sent, kept, columns, order):
    rows, depth = hidden.shape

    def kernel(t_ref, hidden_ref, weight_ref, after_ref, *out_refs):
        product = jnp.dot(hidden_ref[...], weight_ref[...], preferred_element_type=jnp.float32)
        for i in range(len(sent)):

            @pl.when(pl.program_id(0) == i)
            def _():
                out_refs[i][0] = product.astype(jnp.bfloat16)

        if kept:

            @pl.when(pl.program_id(0) >= len(sent))
            def _():
                out_refs[-1][0] = product

    def block(b, t_ref):
        j = jnp.where(
            b < len(sent),
            (sent[0] if sent else 0) - 2 * b,
            (kept[0] if kept else 0) - 2 * (b - len(sent)),
        )
        return 0, t_ref[0] ^ j

    out_shape = [jax.ShapeDtypeStruct((1, rows, columns), jnp.bfloat16)] * len(sent)
    out_specs = [pl.BlockSpec((1, rows, columns), lambda b, _: (0, 0, 0))] * len(sent)
    if kept:
        out_shape.append(jax.ShapeDtypeStruct((len(kept), rows, columns), jnp.float32))
        out_specs.append(
            pl.BlockSpec((1, rows, columns), lambda b, _: (jnp.maximum(b - len(sent), 0), 0, 0))
        )
    outs = pl.pallas_call(
        kernel,
        name="products",
        out_shape=out_shape,
        grid_spec=pltpu.PrefetchScalarGridSpec(
            num_scalar_prefetch=1,
            grid=(len(sent) + len(kept),),
            in_specs=[
                pl.BlockSpec((rows, depth), lambda b, _: (0, 0)),
                pl.BlockSpec((depth, columns), block),
                ANY,
            ],
            out_specs=out_specs,
        ),
        compiler_params=PARAMS,
        cost_estimate=COST,
    )(t.reshape(1), hidden, weight, order.last)
    order.last = outs[-1]
    return outs


def pack_factors(first, second, tp, y):
    rank = first.shape[0]
    widths = [first.shape[1] // (2 * tp), second.shape[1] // (2 * tp)]
    if widths[0] % 128 or widths[1] % 128:
        parts = [
            lax.dynamic_index_in_dim(
                source.reshape(rank, tp, 2, width), y, 2, keepdims=False
            ).transpose(1, 0, 2)
            for source, width in zip((first, second), widths)
        ]
        return jnp.concatenate(parts, axis=2)
    places = [pl.ds(0, widths[0]), pl.ds(widths[0], widths[1])]

    def kernel(y_ref, first_ref, second_ref, out_ref, buffer, in_sem, out_sem):
        def fetch(i, which):
            width = widths[which]
            start = pl.multiple_of((2 * i + y_ref[0]) * width, 128)
            return pltpu.make_async_copy(
                (first_ref, second_ref)[which].at[:, pl.ds(start, width)],
                buffer.at[i, :, places[which]],
                in_sem.at[i, which],
            )

        def store(i):
            return pltpu.make_async_copy(buffer.at[i], out_ref.at[i], out_sem.at[i])

        for i in range(tp):
            for which in range(2):
                fetch(i, which).start()
        for i in range(tp):
            for which in range(2):
                fetch(i, which).wait()
            store(i).start()
        for i in range(tp):
            store(i).wait()

    shape = (tp, rank, sum(widths))
    return pl.pallas_call(
        kernel,
        name="pack_factors",
        out_shape=jax.ShapeDtypeStruct(shape, first.dtype),
        in_specs=[SMEM, ANY, ANY],
        out_specs=ANY,
        scratch_shapes=[
            pltpu.VMEM(shape, first.dtype),
            pltpu.SemaphoreType.DMA((tp, 2)),
            pltpu.SemaphoreType.DMA((tp,)),
        ],
        compiler_params=PARAMS,
        cost_estimate=COST,
    )(y.reshape(1), first, second)


def pack_hidden(hidden, adapter, half, y, order):
    rows = hidden.shape[0]
    if half % 128 or half < rows:
        tags = jnp.pad(adapter[0], (0, -rows % half)).astype(jnp.bfloat16).reshape(-1, half)
        tags = jnp.pad(tags, ((0, TAG_ROWS - tags.shape[0]), (0, 0)))
        return [
            jnp.concatenate(
                [lax.dynamic_slice(hidden, (0, which * half), (rows, half)), tags], axis=0
            )
            for which in (y, 1 - y)
        ]

    def kernel(y_ref, hidden_ref, adapter_ref, after_ref, mine_ref, other_ref, buffer, in_sem, out_sem):
        def fetch(which):
            half_index = y_ref[0] if which == 0 else 1 - y_ref[0]
            return pltpu.make_async_copy(
                hidden_ref.at[:, pl.ds(pl.multiple_of(half_index * half, 128), half)],
                buffer.at[which, pl.ds(0, rows)],
                in_sem.at[which],
            )

        def store(which):
            out_ref = (mine_ref, other_ref)[which]
            return pltpu.make_async_copy(buffer.at[which], out_ref, out_sem.at[which])

        for which in (1, 0):
            fetch(which).start()
        tags = adapter_ref[...].astype(jnp.float32).astype(hidden.dtype)
        for which in (1, 0):
            buffer[which, rows:, :rows] = jnp.broadcast_to(tags, (TAG_ROWS, rows))
        for which in (1, 0):
            fetch(which).wait()
            store(which).start()
        for which in (1, 0):
            store(which).wait()

    shape = jax.ShapeDtypeStruct((rows + TAG_ROWS, half), hidden.dtype)
    mine, other = pl.pallas_call(
        kernel,
        name="pack_hidden",
        out_shape=[shape, shape],
        in_specs=[SMEM, ANY, VMEM, ANY],
        out_specs=[ANY, ANY],
        scratch_shapes=[
            pltpu.VMEM((2, rows + TAG_ROWS, half), hidden.dtype),
            pltpu.SemaphoreType.DMA((2,)),
            pltpu.SemaphoreType.DMA((2,)),
        ],
        compiler_params=PARAMS,
        cost_estimate=COST,
    )(y.reshape(1), hidden, adapter, order.last)
    order.last = mine
    return mine, other


def latent_terms(factors, half, blocks, rows, rank, g, order):
    count = factors.shape[0]
    tp = count // rank
    pairs = len(blocks) // 2

    def term(factor, rows_held, adapter, core):
        full = lax.dot_general(
            factor, rows_held, (((1,), (1,)), ((), ())), preferred_element_type=jnp.float32
        )
        total = jnp.zeros((rank, rows), jnp.float32)
        for place in range(tp):
            total += jnp.where(
                adapter == place * 2 + core, full[place * rank : (place + 1) * rank], 0.0
            )
        return total

    if half % 128 or half < rows:
        outs = [
            term(
                factors[:, :half],
                block[:rows],
                block[rows:].reshape(-1)[:rows][None].astype(jnp.int32),
                g,
            )
            for block in blocks
        ]
        return jnp.stack(outs[:pairs]), jnp.stack(outs[pairs:]), factors[:, half:]

    def kernel(g_ref, factors_ref, *refs):
        block_refs, out_refs = refs[: len(blocks)], refs[len(blocks) + 1 :]
        for i, block_ref in enumerate(block_refs):
            tag = block_ref[rows:, :rows].astype(jnp.float32)[0:1].astype(jnp.int32)
            out_refs[i // pairs][i % pairs] = term(
                factors_ref[:, :half], block_ref[:rows, :], tag, g_ref[0]
            )
        out_refs[-1][...] = factors_ref[:, half:]

    outs = pl.pallas_call(
        kernel,
        name="latent_terms",
        out_shape=[jax.ShapeDtypeStruct((pairs, rank, rows), jnp.float32)] * 2
        + [jax.ShapeDtypeStruct((count, factors.shape[1] - half), factors.dtype)],
        in_specs=[SMEM, VMEM] + [VMEM] * len(blocks) + [ANY],
        out_specs=[VMEM] * 3,
        compiler_params=PARAMS,
        cost_estimate=COST,
    )(g.reshape(1), factors, *blocks, order.last)
    order.last = outs[0]
    return outs


def block_specs(blocks):
    return [
        pl.BlockSpec((1, *array.shape[1:]), lambda b, i=i: (i, 0, 0)) for array, i in blocks
    ]


def fold(sums, order, pair=()):
    blocks = [block for terms in sums for block in terms]
    shape = blocks[0][0].shape[1:]

    def kernel(*refs):
        at = 0
        outs = refs[len(blocks) + len(pair) + 1 :]
        for out_ref, terms in zip(outs, sums):
            total = refs[at][0]
            for ref in refs[at + 1 : at + len(terms)]:
                total += ref[0].astype(jnp.float32)
            out_ref[0] = total.astype(jnp.bfloat16)
            at += len(terms)
        if pair:
            count = pair[0].shape[0]
            outs[-1][:count] = refs[at][...]
            outs[-1][count:] = refs[at + 1][...]

    out_shape = [jax.ShapeDtypeStruct((1, *shape), jnp.bfloat16)] * len(sums)
    out_specs = [pl.BlockSpec((1, *shape), lambda b: (0, 0, 0))] * len(sums)
    if pair:
        count, width = pair[0].shape
        out_shape.append(jax.ShapeDtypeStruct((2 * count, width), pair[0].dtype))
        out_specs.append(pl.BlockSpec((2 * count, width), lambda b: (0, 0)))
    outs = pl.pallas_call(
        kernel,
        name="fold",
        grid=(1,),
        out_shape=out_shape,
        in_specs=block_specs(blocks)
        + [pl.BlockSpec(array.shape, lambda b: (0, 0)) for array in pair]
        + [ANY],
        out_specs=out_specs,
        compiler_params=PARAMS,
        cost_estimate=COST,
    )(*[array for array, _ in blocks], *pair, order.last)
    order.last = outs[0]
    return outs


def relay(array, *after):
    def kernel(*refs):
        del refs

    return pl.pallas_call(
        kernel,
        name="relay",
        out_shape=jax.ShapeDtypeStruct(array.shape, array.dtype),
        in_specs=[ANY] * (1 + len(after)),
        out_specs=ANY,
        input_output_aliases={0: 0},
        compiler_params=PARAMS,
        cost_estimate=COST,
    )(array, *after)


def finish(latents, adapter, seconds, blocks, y, g):
    rows, columns = blocks[0][0].shape[1:]
    rank = latents[0].shape[0]
    tp = seconds[0].shape[0] // rank
    half = columns // 2

    def spread(held, ids, core):
        held = held.astype(jnp.bfloat16).astype(jnp.float32)
        return jnp.concatenate(
            [jnp.where(ids == place * 2 + core, held, jnp.zeros_like(held)) for place in range(tp)],
            axis=0,
        ).astype(jnp.bfloat16)

    def product(left, right):
        return lax.dot_general(
            left, right, (((0,), (0,)), ((), ())), preferred_element_type=jnp.float32
        )

    def total_of(parts):
        total = parts[0]
        for part in parts[1:]:
            total = total + part.astype(jnp.float32)
        return total

    if half % 128:
        latent = total_of(latents)
        near, far = spread(latent, adapter, g), spread(latent, adapter, 1 - g)
        mine = product(near, seconds[0]) + product(far, seconds[1])
        other = product(near, seconds[2]) + product(far, seconds[3])
        delta = jnp.where(
            y == 0,
            jnp.concatenate([mine, other], axis=1),
            jnp.concatenate([other, mine], axis=1),
        )
        total = delta.astype(jnp.bfloat16).astype(jnp.float32)
        for array, i in blocks:
            total = total + array[i].astype(jnp.float32)
        return total.astype(jnp.bfloat16)

    def kernel(y_ref, g_ref, *refs):
        latent_refs, adapter_ref, refs = refs[: len(latents)], refs[len(latents)], refs[len(latents) + 1 :]
        latent = total_of([latent_ref[...] for latent_ref in latent_refs])
        second_refs, block_refs, out_ref = refs[:4], refs[4:-1], refs[-1]
        near = spread(latent, adapter_ref[...], g_ref[0])
        far = spread(latent, adapter_ref[...], 1 - g_ref[0])
        for which in range(2):
            index = y_ref[0] if which == 0 else 1 - y_ref[0]
            lanes = pl.ds(pl.multiple_of(index * half, 128), half)
            delta = product(near, second_refs[2 * which][...])
            delta += product(far, second_refs[2 * which + 1][...])
            total = block_refs[0][0, :, lanes]
            for block_ref in block_refs[1:]:
                total += block_ref[0, :, lanes].astype(jnp.float32)
            total += delta.astype(jnp.bfloat16).astype(jnp.float32)
            out_ref[:, lanes] = total.astype(jnp.bfloat16)

    whole = lambda array: pl.BlockSpec(array.shape, lambda b: (0,) * array.ndim)
    return pl.pallas_call(
        kernel,
        name="finish",
        grid=(1,),
        out_shape=jax.ShapeDtypeStruct((rows, columns), jnp.bfloat16),
        in_specs=[SMEM, SMEM]
        + [whole(array) for array in (*latents, adapter, *seconds)]
        + block_specs(blocks),
        out_specs=pl.BlockSpec((rows, columns), lambda b: (0, 0)),
        compiler_params=PARAMS,
        cost_estimate=COST,
    )(y.reshape(1), g.reshape(1), *latents, adapter, *seconds, *[array for array, _ in blocks])


def local(
    hidden, row_adapter_index, down_projection_weight, adapter_first_factor, adapter_second_factor
):
    tp = lax.axis_size("tp")
    t = lax.axis_index("tp")
    y = lax.axis_index("rep")
    g = lax.axis_index("grp")
    rows, depth = hidden.shape
    rank = adapter_first_factor.shape[2]
    columns = down_projection_weight.shape[1] // tp
    half = depth // 2
    adapter = row_adapter_index.T

    def across(array, step):
        return lax.ppermute(array, "tp", [(i, i ^ step) for i in range(tp)])

    factors = pack_factors(adapter_first_factor[0].T, adapter_second_factor[0], tp, y)
    order = Order(factors)
    factors = lax.all_to_all(factors, "tp", split_axis=0, concat_axis=0, tiled=True)
    factors = factors.reshape(tp * rank, factors.shape[2])
    mine, other = pack_hidden(hidden, adapter, half, y, order)
    from_rep = lax.ppermute(other, "rep", SWAP)
    from_grp = lax.ppermute(mine, "grp", SWAP)
    from_both = lax.ppermute(other, ("rep", "grp"), [(i, 3 - i) for i in range(4)])

    terms = {j: [] for j in range(0, tp, 2)}

    def multiply(sent, kept):
        outs = block_products(hidden, down_projection_weight, t, sent, kept, columns, order)
        for i, j in enumerate(kept):
            terms[j].insert(0, (outs[-1], i))
        for j, out in zip(sent, outs):
            terms[j ^ 1].append((across(out, 1), 0))

    def pass_on(items, pair=()):
        outs = fold([terms[j] for _, j in items], order, pair)
        for (step, j), out in zip(items, outs):
            terms[j ^ step].append((across(out, step), 0))
        return outs[-1]

    odd = list(range(tp - 1, 0, -2))
    stages = []
    step = 2
    while step < tp:
        stages.append([(step, j) for j in range(tp - step, 0, -2 * step)])
        step *= 2

    multiply(odd[:1], [])
    multiply(odd[1:2], [odd[0] - 1])
    multiply(odd[2:], [j - 1 for j in odd[1:]])
    pass_on(stages[0][:1])

    blocks = [mine, from_grp, from_rep, from_both]
    near, away, second = latent_terms(factors, half, blocks, rows, rank, g, order)
    got = lax.ppermute(away, "rep", SWAP)
    near = relay(near, got)
    order.last = near
    rest = [stages[0][1:], *stages[1:]]
    if tp <= 8:
        rest = [[item] for items in reversed(rest) for item in items]
    for items in rest:
        pass_on(items)

    def inner(near, got):
        held = near + got
        latent = held[0] + lax.ppermute(held[1], "grp", SWAP)
        step = 1
        while 4 * step < tp:
            latent = latent + across(latent, step)
            step *= 2
        return latent

    def outer(latent):
        step = tp // 4
        sent = latent.astype(jnp.bfloat16)
        return [across(sent, i * step) for i in range(1, 4)]

    def swap(*arrays):
        return [lax.ppermute(array, "grp", SWAP) for array in arrays]

    def inner_beside(near, got, second):
        other = lax.ppermute(second, "rep", SWAP)
        return lax.cond(t < tp, inner, lambda near, got: near[0], near, got), other

    second = relay(second, order.last)
    latent, second_other = lax.cond(
        t < tp,
        inner_beside,
        lambda near, got, second: (near[0], second),
        near,
        got,
        second,
    )
    kept, (r, i), (late, k), *others = terms[0]
    r = relay(r, latent)
    second_other = relay(second_other, r)
    twins = lax.cond(t < tp, swap, lambda *arrays: list(arrays), second, second_other)
    latent = relay(latent, twins[1])
    got = lax.cond(t < tp, outer, lambda latent: [latent.astype(jnp.bfloat16)] * 3, latent)
    latents = [latent, *got]
    seconds = [second, twins[0], second_other, twins[1]]
    blocks = [kept, (r, i), (relay(late, got[2]), k), *others]
    return finish(latents, adapter, seconds, blocks, y, g)


def solution(mesh):
    return jax.shard_map(
        local,
        mesh=mesh,
        in_specs=(
            P(("rep", "grp"), "tp"),
            P(("rep", "grp"), None),
            P("tp", None),
            P(("tp", "grp"), None, None),
            P(("tp", "grp"), None, None),
        ),
        out_specs=P(("rep", "grp"), "tp"),
        check_vma=False,
    )
```

```python
import jax
import jax.numpy as jnp
from jax import lax
from jax.experimental import pallas as pl
from jax.experimental.pallas import tpu as pltpu
from jax.sharding import PartitionSpec as P

SWAP = ((0, 1), (1, 0))
ANY = pl.BlockSpec(memory_space=pl.ANY)
VMEM = pl.BlockSpec(memory_space=pltpu.VMEM)
SMEM = pl.BlockSpec(memory_space=pltpu.SMEM)
TAG_ROWS = 16
COST = pl.CostEstimate(flops=1, bytes_accessed=1, transcendentals=0)
PARAMS = pltpu.CompilerParams(vmem_limit_bytes=64 * 2**20)


class Order:
    def __init__(self, array):
        self.last = array


def block_products(hidden, weight, t, sent, kept, columns, order):
    rows, depth = hidden.shape

    def kernel(t_ref, hidden_ref, weight_ref, after_ref, *out_refs):
        product = jnp.dot(hidden_ref[...], weight_ref[...], preferred_element_type=jnp.float32)
        for i in range(len(sent)):

            @pl.when(pl.program_id(0) == i)
            def _():
                out_refs[i][0] = product.astype(jnp.bfloat16)

        if kept:

            @pl.when(pl.program_id(0) >= len(sent))
            def _():
                out_refs[-1][0] = product

    def block(b, t_ref):
        j = jnp.where(
            b < len(sent),
            (sent[0] if sent else 0) - 2 * b,
            (kept[0] if kept else 0) - 2 * (b - len(sent)),
        )
        return 0, t_ref[0] ^ j

    out_shape = [jax.ShapeDtypeStruct((1, rows, columns), jnp.bfloat16)] * len(sent)
    out_specs = [pl.BlockSpec((1, rows, columns), lambda b, _: (0, 0, 0))] * len(sent)
    if kept:
        out_shape.append(jax.ShapeDtypeStruct((len(kept), rows, columns), jnp.float32))
        out_specs.append(
            pl.BlockSpec((1, rows, columns), lambda b, _: (jnp.maximum(b - len(sent), 0), 0, 0))
        )
    outs = pl.pallas_call(
        kernel,
        name="products",
        out_shape=out_shape,
        grid_spec=pltpu.PrefetchScalarGridSpec(
            num_scalar_prefetch=1,
            grid=(len(sent) + len(kept),),
            in_specs=[
                pl.BlockSpec((rows, depth), lambda b, _: (0, 0)),
                pl.BlockSpec((depth, columns), block),
                ANY,
            ],
            out_specs=out_specs,
        ),
        compiler_params=PARAMS,
        cost_estimate=COST,
    )(t.reshape(1), hidden, weight, order.last)
    order.last = outs[-1]
    return outs


def pack_factors(first, second, tp, y):
    rank = first.shape[0]
    widths = [first.shape[1] // (2 * tp), second.shape[1] // (2 * tp)]
    if widths[0] % 128 or widths[1] % 128:
        parts = [
            lax.dynamic_index_in_dim(
                source.reshape(rank, tp, 2, width), y, 2, keepdims=False
            ).transpose(1, 0, 2)
            for source, width in zip((first, second), widths)
        ]
        return jnp.concatenate(parts, axis=2)
    places = [pl.ds(0, widths[0]), pl.ds(widths[0], widths[1])]

    def kernel(y_ref, first_ref, second_ref, out_ref, buffer, in_sem, out_sem):
        def fetch(i, which):
            width = widths[which]
            start = pl.multiple_of((2 * i + y_ref[0]) * width, 128)
            return pltpu.make_async_copy(
                (first_ref, second_ref)[which].at[:, pl.ds(start, width)],
                buffer.at[i, :, places[which]],
                in_sem.at[i, which],
            )

        def store(i):
            return pltpu.make_async_copy(buffer.at[i], out_ref.at[i], out_sem.at[i])

        for i in range(tp):
            for which in range(2):
                fetch(i, which).start()
        for i in range(tp):
            for which in range(2):
                fetch(i, which).wait()
            store(i).start()
        for i in range(tp):
            store(i).wait()

    shape = (tp, rank, sum(widths))
    return pl.pallas_call(
        kernel,
        name="pack_factors",
        out_shape=jax.ShapeDtypeStruct(shape, first.dtype),
        in_specs=[SMEM, ANY, ANY],
        out_specs=ANY,
        scratch_shapes=[
            pltpu.VMEM(shape, first.dtype),
            pltpu.SemaphoreType.DMA((tp, 2)),
            pltpu.SemaphoreType.DMA((tp,)),
        ],
        compiler_params=PARAMS,
        cost_estimate=COST,
    )(y.reshape(1), first, second)


def pack_hidden(hidden, adapter, half, y, order):
    rows = hidden.shape[0]
    if half % 128 or half < rows:
        tags = jnp.pad(adapter[0], (0, -rows % half)).astype(jnp.bfloat16).reshape(-1, half)
        tags = jnp.pad(tags, ((0, TAG_ROWS - tags.shape[0]), (0, 0)))
        return [
            jnp.concatenate(
                [lax.dynamic_slice(hidden, (0, which * half), (rows, half)), tags], axis=0
            )
            for which in (y, 1 - y)
        ]

    def kernel(y_ref, hidden_ref, adapter_ref, after_ref, mine_ref, other_ref, buffer, in_sem, out_sem):
        def fetch(which):
            half_index = y_ref[0] if which == 0 else 1 - y_ref[0]
            return pltpu.make_async_copy(
                hidden_ref.at[:, pl.ds(pl.multiple_of(half_index * half, 128), half)],
                buffer.at[which, pl.ds(0, rows)],
                in_sem.at[which],
            )

        def store(which):
            out_ref = (mine_ref, other_ref)[which]
            return pltpu.make_async_copy(buffer.at[which], out_ref, out_sem.at[which])

        for which in (1, 0):
            fetch(which).start()
        tags = adapter_ref[...].astype(jnp.float32).astype(hidden.dtype)
        for which in (1, 0):
            buffer[which, rows:, :rows] = jnp.broadcast_to(tags, (TAG_ROWS, rows))
        for which in (1, 0):
            fetch(which).wait()
            store(which).start()
        for which in (1, 0):
            store(which).wait()

    shape = jax.ShapeDtypeStruct((rows + TAG_ROWS, half), hidden.dtype)
    mine, other = pl.pallas_call(
        kernel,
        name="pack_hidden",
        out_shape=[shape, shape],
        in_specs=[SMEM, ANY, VMEM, ANY],
        out_specs=[ANY, ANY],
        scratch_shapes=[
            pltpu.VMEM((2, rows + TAG_ROWS, half), hidden.dtype),
            pltpu.SemaphoreType.DMA((2,)),
            pltpu.SemaphoreType.DMA((2,)),
        ],
        compiler_params=PARAMS,
        cost_estimate=COST,
    )(y.reshape(1), hidden, adapter, order.last)
    order.last = mine
    return mine, other


def latent_terms(factors, half, blocks, rows, rank, g, order):
    count = factors.shape[0]
    tp = count // rank
    pairs = len(blocks) // 2

    def term(factor, rows_held, adapter, core):
        full = lax.dot_general(
            factor, rows_held, (((1,), (1,)), ((), ())), preferred_element_type=jnp.float32
        )
        total = jnp.zeros((rank, rows), jnp.float32)
        for place in range(tp):
            total += jnp.where(
                adapter == place * 2 + core, full[place * rank : (place + 1) * rank], 0.0
            )
        return total

    if half % 128 or half < rows:
        outs = [
            term(
                factors[:, :half],
                block[:rows],
                block[rows:].reshape(-1)[:rows][None].astype(jnp.int32),
                g,
            )
            for block in blocks
        ]
        return jnp.stack(outs[:pairs]), jnp.stack(outs[pairs:]), factors[:, half:]

    def kernel(g_ref, factors_ref, *refs):
        block_refs, out_refs = refs[: len(blocks)], refs[len(blocks) + 1 :]
        for i, block_ref in enumerate(block_refs):
            tag = block_ref[rows:, :rows].astype(jnp.float32)[0:1].astype(jnp.int32)
            out_refs[i // pairs][i % pairs] = term(
                factors_ref[:, :half], block_ref[:rows, :], tag, g_ref[0]
            )
        out_refs[-1][...] = factors_ref[:, half:]

    outs = pl.pallas_call(
        kernel,
        name="latent_terms",
        out_shape=[jax.ShapeDtypeStruct((pairs, rank, rows), jnp.float32)] * 2
        + [jax.ShapeDtypeStruct((count, factors.shape[1] - half), factors.dtype)],
        in_specs=[SMEM, VMEM] + [VMEM] * len(blocks) + [ANY],
        out_specs=[VMEM] * 3,
        compiler_params=PARAMS,
        cost_estimate=COST,
    )(g.reshape(1), factors, *blocks, order.last)
    order.last = outs[0]
    return outs


def block_specs(blocks):
    return [
        pl.BlockSpec((1, *array.shape[1:]), lambda b, i=i: (i, 0, 0)) for array, i in blocks
    ]


def fold(sums, order, pair=()):
    blocks = [block for terms in sums for block in terms]
    shape = blocks[0][0].shape[1:]

    def kernel(*refs):
        at = 0
        outs = refs[len(blocks) + len(pair) + 1 :]
        for out_ref, terms in zip(outs, sums):
            total = refs[at][0]
            for ref in refs[at + 1 : at + len(terms)]:
                total += ref[0].astype(jnp.float32)
            out_ref[0] = total.astype(jnp.bfloat16)
            at += len(terms)
        if pair:
            count = pair[0].shape[0]
            outs[-1][:count] = refs[at][...]
            outs[-1][count:] = refs[at + 1][...]

    out_shape = [jax.ShapeDtypeStruct((1, *shape), jnp.bfloat16)] * len(sums)
    out_specs = [pl.BlockSpec((1, *shape), lambda b: (0, 0, 0))] * len(sums)
    if pair:
        count, width = pair[0].shape
        out_shape.append(jax.ShapeDtypeStruct((2 * count, width), pair[0].dtype))
        out_specs.append(pl.BlockSpec((2 * count, width), lambda b: (0, 0)))
    outs = pl.pallas_call(
        kernel,
        name="fold",
        grid=(1,),
        out_shape=out_shape,
        in_specs=block_specs(blocks)
        + [pl.BlockSpec(array.shape, lambda b: (0, 0)) for array in pair]
        + [ANY],
        out_specs=out_specs,
        compiler_params=PARAMS,
        cost_estimate=COST,
    )(*[array for array, _ in blocks], *pair, order.last)
    order.last = outs[0]
    return outs


def relay(array, *after):
    def kernel(*refs):
        del refs

    return pl.pallas_call(
        kernel,
        name="relay",
        out_shape=jax.ShapeDtypeStruct(array.shape, array.dtype),
        in_specs=[ANY] * (1 + len(after)),
        out_specs=ANY,
        input_output_aliases={0: 0},
        compiler_params=PARAMS,
        cost_estimate=COST,
    )(array, *after)


def finish(latents, adapter, seconds, blocks, y, g):
    rows, columns = blocks[0][0].shape[1:]
    rank = latents[0].shape[0]
    tp = seconds[0].shape[0] // rank
    half = columns // 2

    def spread(held, ids, core):
        held = held.astype(jnp.bfloat16).astype(jnp.float32)
        return jnp.concatenate(
            [jnp.where(ids == place * 2 + core, held, jnp.zeros_like(held)) for place in range(tp)],
            axis=0,
        ).astype(jnp.bfloat16)

    def product(left, right):
        return lax.dot_general(
            left, right, (((0,), (0,)), ((), ())), preferred_element_type=jnp.float32
        )

    def total_of(parts):
        total = parts[0]
        for part in parts[1:]:
            total = total + part.astype(jnp.float32)
        return total

    if half % 128:
        latent = total_of(latents)
        near, far = spread(latent, adapter, g), spread(latent, adapter, 1 - g)
        mine = product(near, seconds[0]) + product(far, seconds[1])
        other = product(near, seconds[2]) + product(far, seconds[3])
        delta = jnp.where(
            y == 0,
            jnp.concatenate([mine, other], axis=1),
            jnp.concatenate([other, mine], axis=1),
        )
        total = delta.astype(jnp.bfloat16).astype(jnp.float32)
        for array, i in blocks:
            total = total + array[i].astype(jnp.float32)
        return total.astype(jnp.bfloat16)

    def kernel(y_ref, g_ref, *refs):
        latent_refs, adapter_ref, refs = refs[: len(latents)], refs[len(latents)], refs[len(latents) + 1 :]
        latent = total_of([latent_ref[...] for latent_ref in latent_refs])
        second_refs, block_refs, out_ref = refs[:4], refs[4:-1], refs[-1]
        near = spread(latent, adapter_ref[...], g_ref[0])
        far = spread(latent, adapter_ref[...], 1 - g_ref[0])
        for which in range(2):
            index = y_ref[0] if which == 0 else 1 - y_ref[0]
            lanes = pl.ds(pl.multiple_of(index * half, 128), half)
            delta = product(near, second_refs[2 * which][...])
            delta += product(far, second_refs[2 * which + 1][...])
            total = block_refs[0][0, :, lanes]
            for block_ref in block_refs[1:]:
                total += block_ref[0, :, lanes].astype(jnp.float32)
            total += delta.astype(jnp.bfloat16).astype(jnp.float32)
            out_ref[:, lanes] = total.astype(jnp.bfloat16)

    whole = lambda array: pl.BlockSpec(array.shape, lambda b: (0,) * array.ndim)
    return pl.pallas_call(
        kernel,
        name="finish",
        grid=(1,),
        out_shape=jax.ShapeDtypeStruct((rows, columns), jnp.bfloat16),
        in_specs=[SMEM, SMEM]
        + [whole(array) for array in (*latents, adapter, *seconds)]
        + block_specs(blocks),
        out_specs=pl.BlockSpec((rows, columns), lambda b: (0, 0)),
        compiler_params=PARAMS,
        cost_estimate=COST,
    )(y.reshape(1), g.reshape(1), *latents, adapter, *seconds, *[array for array, _ in blocks])


def local(
    hidden, row_adapter_index, down_projection_weight, adapter_first_factor, adapter_second_factor
):
    tp = lax.axis_size("tp")
    t = lax.axis_index("tp")
    y = lax.axis_index("rep")
    g = lax.axis_index("grp")
    rows, depth = hidden.shape
    rank = adapter_first_factor.shape[2]
    columns = down_projection_weight.shape[1] // tp
    half = depth // 2
    adapter = row_adapter_index.T

    def across(array, step):
        return lax.ppermute(array, "tp", [(i, i ^ step) for i in range(tp)])

    factors = pack_factors(adapter_first_factor[0].T, adapter_second_factor[0], tp, y)
    order = Order(factors)
    factors = lax.all_to_all(factors, "tp", split_axis=0, concat_axis=0, tiled=True)
    factors = factors.reshape(tp * rank, factors.shape[2])
    mine, other = pack_hidden(hidden, adapter, half, y, order)
    from_rep = lax.ppermute(other, "rep", SWAP)
    from_grp = lax.ppermute(mine, "grp", SWAP)
    from_both = lax.ppermute(other, ("rep", "grp"), [(i, 3 - i) for i in range(4)])

    terms = {j: [] for j in range(0, tp, 2)}

    def multiply(sent, kept):
        outs = block_products(hidden, down_projection_weight, t, sent, kept, columns, order)
        for i, j in enumerate(kept):
            terms[j].insert(0, (outs[-1], i))
        for j, out in zip(sent, outs):
            terms[j ^ 1].append((across(out, 1), 0))

    def pass_on(items, pair=()):
        outs = fold([terms[j] for _, j in items], order, pair)
        for (step, j), out in zip(items, outs):
            terms[j ^ step].append((across(out, step), 0))
        return outs[-1]

    odd = list(range(tp - 1, 0, -2))
    stages = []
    step = 2
    while step < tp:
        stages.append([(step, j) for j in range(tp - step, 0, -2 * step)])
        step *= 2

    multiply(odd[:1], [])
    multiply(odd[1:2], [odd[0] - 1])
    multiply(odd[2:], [j - 1 for j in odd[1:]])
    pass_on(stages[0][:1])

    blocks = [mine, from_grp, from_rep, from_both]
    near, away, second = latent_terms(factors, half, blocks, rows, rank, g, order)
    got = lax.ppermute(away, "rep", SWAP)
    near = relay(near, got)
    order.last = near
    rest = [stages[0][1:], *stages[1:]]
    if tp <= 8:
        rest = [[item] for items in reversed(rest) for item in items]
    for items in rest:
        pass_on(items)

    def swap(*arrays):
        return [lax.ppermute(array, "grp", SWAP) for array in arrays]

    def inner(near, got):
        held = near + got
        latent = held[0] + lax.ppermute(held[1], "grp", SWAP)
        step = 1
        while 4 * step < tp:
            latent = latent + across(latent, step)
            step *= 2
        return latent

    def outer(latent):
        step = tp // 4
        sent = latent.astype(jnp.bfloat16)
        return [across(sent, i * step) for i in range(1, 4)]

    def inner_beside(near, got, second):
        other = lax.ppermute(second, "rep", SWAP)
        held = lax.cond(t < tp, swap, lambda *arrays: list(arrays), second)
        return lax.cond(t < tp, inner, lambda near, got: near[0], near, got), other, held[0]

    second = relay(second, order.last)
    latent, second_other, twin = lax.cond(
        t < tp,
        inner_beside,
        lambda near, got, second: (near[0], second, second),
        near,
        got,
        second,
    )
    kept, (r, i), (late, k), *others = terms[0]
    r = relay(r, latent)
    second_other = relay(second_other, r)
    twins = [twin, *lax.cond(t < tp, swap, lambda *arrays: list(arrays), second_other)]
    latent = relay(latent, twins[1])
    got = lax.cond(t < tp, outer, lambda latent: [latent.astype(jnp.bfloat16)] * 3, latent)
    latents = [latent, *got]
    seconds = [second, twins[0], second_other, twins[1]]
    blocks = [kept, (r, i), (relay(late, got[2]), k), *others]
    return finish(latents, adapter, seconds, blocks, y, g)


def solution(mesh):
    return jax.shard_map(
        local,
        mesh=mesh,
        in_specs=(
            P(("rep", "grp"), "tp"),
            P(("rep", "grp"), None),
            P("tp", None),
            P(("tp", "grp"), None, None),
            P(("tp", "grp"), None, None),
        ),
        out_specs=P(("rep", "grp"), "tp"),
        check_vma=False,
    )
```
